32 devices in a mesh: section: 2 (over x), fsdp: 4 (over y, core), dp: 4 (over z).
Axes of the slice: x: 2, y: 2, z: 4, core: 2. Of those that a mesh axis runs over, the one named last changes fastest.
Arguments:
- ends: bfloat16 [2, 2, 4, 1024, 2048], P('section', None, 'dp', 'fsdp'), may hold values from -6 to 6
- positions: int32 [2, 4, 1024], P(None, 'dp', 'fsdp'), may hold values from 0 to 4093, as said below
- attn_gain: bfloat16 [2, 2048], P('section', 'fsdp'), may hold values from 0.5 to 1.5
- w_query: bfloat16 [2, 2048, 2048], P('section', 'fsdp'), may hold values from -0.125 to 0.125
- w_key: bfloat16 [2, 2048, 512], P('section', 'fsdp'), may hold values from -0.125 to 0.125
- w_value: bfloat16 [2, 2048, 512], P('section', 'fsdp'), may hold values from -0.125 to 0.125
- w_out: bfloat16 [2, 2048, 2048], P('section', 'fsdp'), may hold values from -1.5 to 1.5
- mlp_gain: bfloat16 [2, 2048], P('section', 'fsdp'), may hold values from 0.5 to 1.5
- w_gate: bfloat16 [2, 2048, 8192], P('section', 'fsdp'), may hold values from -0.125 to 0.125
- w_up: bfloat16 [2, 2048, 8192], P('section', 'fsdp'), may hold values from -0.125 to 0.125
- w_down: bfloat16 [2, 8192, 2048], P('section', 'fsdp'), may hold values from -0.0625 to 0.0625
Outputs:
- boundary: float32 [2, 2, 4, 1024, 2048], P('section', None, 'dp', 'fsdp')
- grad_attn_gain: float32 [2, 2048], P('section', 'fsdp')
- grad_query: float32 [2, 2048, 2048], P('section', 'fsdp')
- grad_key: float32 [2, 2048, 512], P('section', 'fsdp')
- grad_value: float32 [2, 2048, 512], P('section', 'fsdp')
- grad_out: float32 [2, 2048, 2048], P('section', 'fsdp')
- grad_mlp_gain: float32 [2, 2048], P('section', 'fsdp')
- grad_gate: float32 [2, 2048, 8192], P('section', 'fsdp')
- grad_up: float32 [2, 2048, 8192], P('section', 'fsdp')
- grad_down: float32 [2, 8192, 2048], P('section', 'fsdp')
The draws below stay inside these ranges and needn't reach their ends.
Inputs may be any that keep to these rules, and one draw needn't show every extreme that they name: Within a sequence, positions rise by 1 to 3 from one token to the next; a sequence's first position lies from 0 to 1024.
All inputs are finite; a program needn't handle non-finite values.
Results may differ from the reference program's by a relative error of at most 0.024.
Values may be sent and summed in bfloat16 or wider, within the bound.
No kernel may reach another device: no remote copies, remote signals or barrier semaphores. Data moves between devices by JAX's collectives and lax.ppermute only.
A program may use at most 576 MiB of HBM per device.

```python
import jax
import jax.numpy as jnp
from jax import lax

D = 2048
FF = 8192
Q_HEADS = 32
KV_HEADS = 8
HEAD_DIM = 64
MICRO = 2
LAYERS = 2
LENGTH = 1024
SEQS = 4


def draw_positions(key, part):
    key = jax.random.fold_in(key, 11)
    start_key = jax.random.fold_in(key, 1)
    step_key = jax.random.fold_in(key, 2)
    start = jax.random.randint(start_key, (MICRO, SEQS, 1), 0, LENGTH + 1).astype(jnp.int32)
    start = start.at[0, 0, 0].set(0)
    start = start.at[MICRO - 1, SEQS - 1, 0].set(LENGTH)
    steps = jax.random.randint(step_key, (MICRO, SEQS, LENGTH), 1, 4).astype(jnp.int32)
    steps = steps.at[MICRO - 1, SEQS - 1, :].set(3)
    steps = steps.at[:, :, 0].set(0)
    offsets = jnp.cumsum(steps, axis=-1).astype(jnp.int32)
    return (start + offsets).astype(jnp.int32)


def block_levels(stream_key, dims, split, smallest, high):
    gain = 1.0
    for position, parts in split:
        draws = jax.random.uniform(jax.random.fold_in(jax.random.fold_in(stream_key, 6), position), (parts,), jnp.float32, smallest / len(split), high / len(split))
        gain = gain * jnp.repeat(jnp.exp(draws), dims[position] // parts).reshape((-1,) + (1,) * (len(dims) - 1 - position))
    return gain


def scatter_about(stream_key, extent, scale, bound, split=(), kind=jnp.bfloat16):
    values = scale * jax.random.normal(stream_key, extent, jnp.float32)
    if split:
        values = values * block_levels(stream_key, extent, split, -0.22, 0.18)
    return jnp.clip(values, -bound, bound).astype(kind)


def setup_inputs(seed: int = 0) -> dict:
    key_list = jax.random.split(jax.random.key(seed), 12)
    return {
        "ends": scatter_about(key_list[0], (2, MICRO, SEQS, LENGTH, D), 1.0, 6.0, ((0, 2), (2, 4), (3, 4))),
        "positions": draw_positions(jax.random.fold_in(key_list[11], 71), 0),
        "attn_gain": jnp.clip(1.0 + 0.1 * jax.random.normal(key_list[2], (LAYERS, D), jnp.float32), 0.5, 1.5).astype(jnp.bfloat16),
        "w_query": scatter_about(key_list[3], (LAYERS, D, Q_HEADS * HEAD_DIM), D ** -0.5, 0.125, ((0, 2), (1, 4))),
        "w_key": scatter_about(key_list[4], (LAYERS, D, KV_HEADS * HEAD_DIM), D ** -0.5, 0.125, ((0, 2), (1, 4))),
        "w_value": scatter_about(key_list[5], (LAYERS, D, KV_HEADS * HEAD_DIM), D ** -0.5, 0.125, ((0, 2), (1, 4))),
        "w_out": scatter_about(key_list[6], (LAYERS, Q_HEADS * HEAD_DIM, D), (max(D // 128, 1)) ** -0.5, 1.5, ((0, 2), (1, 4))),
        "mlp_gain": jnp.clip(1.0 + 0.1 * jax.random.normal(key_list[7], (LAYERS, D), jnp.float32), 0.5, 1.5).astype(jnp.bfloat16),
        "w_gate": scatter_about(key_list[8], (LAYERS, D, FF), D ** -0.5, 0.125, ((0, 2), (1, 4))),
        "w_up": scatter_about(key_list[9], (LAYERS, D, FF), D ** -0.5, 0.125, ((0, 2), (1, 4))),
        "w_down": scatter_about(key_list[10], (LAYERS, FF, D), FF ** -0.5, 0.0625, ((0, 2), (1, 4))),
    }


EPSILON = 1e-05
ROPE_THETA = 500000.0

@jax.custom_vjp
def low(v):
    return lax.optimization_barrier(v.astype(jnp.bfloat16)).astype(jnp.float32)

@jax.custom_vjp
def low_back(v):
    return v

def low_keep(v):
    return (low(v), None)

def low_pass(kept, grad):
    return (grad,)

def back_keep(v):
    return (v, None)

def back_low(kept, grad):
    return (low(grad),)
low.defvjp(low_keep, low_pass)
low_back.defvjp(back_keep, back_low)

def precise(left, right):
    return jnp.dot(left, right, precision=lax.Precision.HIGHEST)

def rms_inverse(vector):
    return lax.rsqrt(lax.optimization_barrier(jnp.mean(vector * vector, axis=-1, keepdims=True)) + EPSILON)

def rope_tables(places):
    half_dim = HEAD_DIM // 2
    frequency = jnp.exp(-jnp.log(ROPE_THETA) * 2.0 * jnp.arange(half_dim, dtype=jnp.float32) / HEAD_DIM)
    angles = places.astype(jnp.float32)[:, None] * frequency[None, :]
    return (jnp.cos(angles)[:, None, :], jnp.sin(angles)[:, None, :])

def rotate(heads, cosine_table, sine_table):
    half_dim = heads.shape[-1] // 2
    first = heads[..., :half_dim]
    second = heads[..., half_dim:]
    return jnp.concatenate([first * cosine_table - second * sine_table, second * cosine_table + first * sine_table], axis=-1)

def attend(packed):
    queries, keys_all, values_all = packed
    length = queries.shape[0]
    group_size = Q_HEADS // KV_HEADS
    grouped = queries.reshape(length, KV_HEADS, group_size, HEAD_DIM)
    scores = jnp.einsum('qkgd,skd->kgqs', grouped, keys_all, precision=lax.Precision.HIGHEST) * HEAD_DIM ** (-0.5)
    causal = jnp.arange(length)[:, None] >= jnp.arange(length)[None, :]
    scores = low_back(jnp.where(causal[None, None], scores, -1e+30))
    attn_probs = low(jax.nn.softmax(scores, axis=-1))
    attended = jnp.einsum('kgqs,skd->qkgd', attn_probs, values_all, precision=lax.Precision.HIGHEST)
    return attended.reshape(length, Q_HEADS * HEAD_DIM)

def layer(residual_in, places, weights):
    attn_gain, w_query, w_key, w_value, w_out, mlp_gain, w_gate, w_up, w_down = weights
    tok_rows = residual_in.shape[0]
    normed_attn = low(residual_in * rms_inverse(residual_in) * attn_gain)
    cosine_table, sine_table = rope_tables(places)
    queries = low_back(precise(normed_attn, w_query)).reshape(tok_rows, Q_HEADS, HEAD_DIM)
    keys_local = low_back(precise(normed_attn, w_key)).reshape(tok_rows, KV_HEADS, HEAD_DIM)
    values_local = low(low_back(precise(normed_attn, w_value))).reshape(tok_rows, KV_HEADS, HEAD_DIM)
    queries = low(rotate(queries, cosine_table, sine_table))
    keys_local = low(rotate(keys_local, cosine_table, sine_table))
    seq_count = tok_rows // LENGTH
    attended = lax.map(jax.checkpoint(attend), (queries.reshape(seq_count, LENGTH, Q_HEADS, HEAD_DIM), keys_local.reshape(seq_count, LENGTH, KV_HEADS, HEAD_DIM), values_local.reshape(seq_count, LENGTH, KV_HEADS, HEAD_DIM)))
    attended = low(low_back(attended.reshape(tok_rows, Q_HEADS * HEAD_DIM)))
    residual_mid = residual_in + low_back(precise(attended, w_out))
    normed_mlp = low(residual_mid * rms_inverse(residual_mid) * mlp_gain)
    gate_pre = low_back(precise(normed_mlp, w_gate))
    up_proj = low_back(precise(normed_mlp, w_up))
    hidden_act = low(jax.nn.silu(gate_pre) * up_proj)
    return residual_mid + low_back(precise(hidden_act, w_down))

def reference(ends, positions, attn_gain, w_query, w_key, w_value, w_out, mlp_gain, w_gate, w_up, w_down):
    tokens = ends[0].astype(jnp.float32).reshape(-1, D)
    cotangent = ends[1].astype(jnp.float32).reshape(-1, D)
    places = positions.reshape(-1)
    params = tuple((weight.astype(jnp.float32) for weight in (attn_gain, w_query, w_key, w_value, w_out, mlp_gain, w_gate, w_up, w_down)))

    def forward(inputs, weights):
        current = inputs
        for layer_index in range(LAYERS):
            layer_weights = tuple((weight[layer_index] for weight in weights))
            current = jax.checkpoint(layer)(current, places, layer_weights)
            if layer_index + 1 < LAYERS:
                current = low(low_back(current))
        return current
    result, pullback = jax.vjp(forward, tokens, params)
    grad_tokens, grad_params = pullback(cotangent)
    boundary = jnp.stack([grad_tokens, result]).reshape(ends.shape)
    return (boundary, grad_params[0], grad_params[1], grad_params[2], grad_params[3], grad_params[4], grad_params[5], grad_params[6], grad_params[7], grad_params[8])
```

```python
import jax
import jax.numpy as jnp
from jax import lax
from jax.sharding import PartitionSpec as P

HEAD_DIM = 64
EPSILON = 1e-05
ROPE_THETA = 500000.0
CHUNK_ROWS = 512
CHUNK_COLS = 1024
STREAMS = 2
BF = jnp.bfloat16
F32 = jnp.float32


def dot_plain(left, right):
    return jnp.dot(left, right, preferred_element_type=F32)


def dot_rows(left, right):
    return lax.dot_general(left, right, (((0,), (0,)), ((), ())), preferred_element_type=F32)


def dot_cols(left, right):
    return lax.dot_general(left, right, (((1,), (1,)), ((), ())), preferred_element_type=F32)


def rms_inverse(vector):
    return lax.rsqrt(jnp.mean(vector * vector, axis=-1, keepdims=True) + EPSILON)


def rope_tables(places):
    half_dim = HEAD_DIM // 2
    frequency = jnp.exp(-jnp.log(ROPE_THETA) * 2.0 * jnp.arange(half_dim, dtype=F32) / HEAD_DIM)
    angles = places.astype(F32)[:, None] * frequency[None, :]
    return (jnp.cos(angles)[:, None, :], jnp.sin(angles)[:, None, :])


def rotate(heads, cosine_table, sine_table):
    half_dim = heads.shape[-1] // 2
    first = heads[..., :half_dim]
    second = heads[..., half_dim:]
    return jnp.concatenate(
        [first * cosine_table - second * sine_table, second * cosine_table + first * sine_table],
        axis=-1,
    )


def core_swap(x):
    return lax.ppermute(x, "fsdp", [(0, 1), (1, 0), (2, 3), (3, 2)])


def chip_swap(x):
    return lax.ppermute(x, "fsdp", [(0, 2), (2, 0), (1, 3), (3, 1)])


def after(value, *others):
    return lax.optimization_barrier((value, *others))[0]


def column_block(x, index, width):
    return lax.dynamic_slice_in_dim(x, index * width, width, axis=1)


def swapped_columns(x, shard):
    width = x.shape[1] // 4
    return jnp.concatenate([column_block(x, shard ^ k, width) for k in range(4)], axis=1)


def replica_chain(chunks):
    peers = lax.axis_size("dp")
    place = lax.axis_index("dp")
    root = (peers - 1) // 2
    delay = max(root, peers - 1 - root)
    up_pairs = [(i, i + 1) for i in range(peers - 1)]
    down_pairs = [(i + 1, i) for i in range(peers - 1)]
    shape = chunks[0].shape
    streams = [chunks[q::STREAMS] for q in range(STREAMS)]
    counts = [len(stream) for stream in streams]
    ups = [[] for _ in streams]
    downs = [[] for _ in streams]
    sent = [[] for _ in streams]
    order = []

    def nth(items, index):
        return items[index].astype(F32) if 0 <= index < len(items) else 0.0

    for step in range(max(counts) + 2 * delay):
        for q in range(STREAMS):
            if step >= counts[q] + 2 * delay:
                continue
            own = 0.0
            for position in range(peers):
                if position < root:
                    index = step - position
                elif position == root:
                    index = step - delay
                else:
                    index = step - (peers - 1 - position)
                if 0 <= index < counts[q]:
                    own = jnp.where(place == position, streams[q][index].astype(F32), own)
            from_below = nth(ups[q], step - 1)
            from_above = nth(downs[q], step - 1)
            below_held = nth(ups[q], step - 1 - (delay - root))
            above_held = nth(downs[q], step - 1 - (delay - (peers - 1 - root)))
            total = own + below_held + above_held
            up = jnp.where(place == root, total, from_below + jnp.where(place < root, own, 0.0))
            down = jnp.where(place == root, total, from_above + jnp.where(place > root, own, 0.0))
            up = jnp.broadcast_to(up, shape).astype(BF)
            down = jnp.broadcast_to(down, shape).astype(BF)
            if len(order) > STREAMS:
                up, down = lax.optimization_barrier((up, down, *order[-(STREAMS + 1)]))[:2]
            sent[q].append((up, down))
            if step < counts[q] + 2 * delay - 1:
                ups[q].append(lax.ppermute(up, "dp", up_pairs))
                downs[q].append(lax.ppermute(down, "dp", down_pairs))
                order.append((ups[q][-1], downs[q][-1]))
    distance = jnp.abs(place - root)
    totals = [None] * len(chunks)
    for q in range(STREAMS):
        for index in range(counts[q]):
            total = None
            for hops in range(delay + 1):
                up, down = sent[q][index + delay + hops]
                value = jnp.where(place >= root, up, down)
                total = value if total is None else jnp.where(distance == hops, value, total)
            totals[q + index * STREAMS] = total
    return totals


def gather_weights(w_query, w_key, w_value, w_out, w_gate, w_up, w_down):
    replica = lax.axis_index("dp")
    replicas = lax.axis_size("dp")

    def part(x):
        rows = x.shape[0] // replicas
        return lax.dynamic_slice_in_dim(x, replica * rows, rows, axis=0)

    def spread(x):
        return lax.all_gather(x, "dp", axis=0, tiled=True)

    half = w_down.shape[0] // 2
    qkv = jnp.concatenate([w_query, w_key, w_value], axis=1)
    sends = [part(w_gate), qkv, part(w_up), w_out, w_down[:half], part(w_down[half:])]
    got = []
    for index, send in enumerate(sends):
        if index >= 2:
            send = after(send, got[index - 2])
        got.append(chip_swap(send))
    other_gate = spread(got[0])
    other_up = spread(got[2])
    other_down = spread(got[5])
    table = [
        (qkv, got[1]),
        (w_gate, other_gate),
        (w_out, got[3]),
        (w_up, other_up),
        (w_down[:half], got[4]),
        (w_down[half:], other_down),
    ]
    whole = []
    for own, other in table:
        whole.append((own, core_swap(own), other, core_swap(other)))
    down = []
    for k in range(4):
        down += [whole[4][k], whole[5][k]]
    return tuple(jnp.concatenate(p, axis=0) for p in (*whole[:4], down))


def body(
    ends, positions, attn_gain, w_query, w_key, w_value, w_out, mlp_gain, w_gate, w_up, w_down
):
    shard = lax.axis_index("fsdp")
    first_section = lax.axis_index("section") == 0
    gain_attn = lax.all_gather(attn_gain, "fsdp", axis=1, tiled=True)[0].astype(F32)
    gain_mlp = lax.all_gather(mlp_gain, "fsdp", axis=1, tiled=True)[0].astype(F32)
    mat_qkv, mat_gate, mat_out, mat_up, mat_down = gather_weights(
        w_query[0], w_key[0], w_value[0], w_out[0], w_gate[0], w_up[0], w_down[0]
    )
    tok_rows = ends.shape[3]
    model_width = ends.shape[4]
    length = tok_rows * lax.axis_size("fsdp")
    key_width = w_key.shape[2]
    query_width = w_query.shape[2]
    key_heads = key_width // HEAD_DIM
    query_heads = query_width // HEAD_DIM
    group_size = query_heads // key_heads
    score_scale = HEAD_DIM ** (-0.5)
    ends_local = ends[0, :, 0]
    places_local = positions[:, 0]
    query_index = shard * tok_rows + jnp.arange(tok_rows, dtype=jnp.int32)
    causal = query_index[:, None] >= jnp.arange(length, dtype=jnp.int32)[None, :]
    tables = [rope_tables(places_local[micro]) for micro in range(2)]

    def pick(first, second):
        return jax.tree.map(lambda left, right: jnp.where(first_section, left, right), first, second)

    def split_heads(queries, keys_all, values_all):
        return (
            queries.reshape(tok_rows, key_heads, group_size, HEAD_DIM).transpose(1, 0, 2, 3),
            keys_all.reshape(length, key_heads, HEAD_DIM).transpose(1, 0, 2),
            values_all.reshape(length, key_heads, HEAD_DIM).transpose(1, 0, 2),
        )

    def masked_scores(query_block, key_block):
        scores = (
            jnp.einsum("rgd,sd->grs", query_block, key_block, preferred_element_type=F32)
            * score_scale
        )
        return jnp.where(causal[None], scores, -1e30)

    def attend_group(packed):
        query_block, key_block, value_block = packed
        scores = masked_scores(query_block, key_block)
        row_max = jnp.max(scores, axis=-1, keepdims=True)
        exp_scores = jnp.exp(scores - row_max)
        row_total = jnp.sum(exp_scores, axis=-1, keepdims=True)
        attn_probs = (exp_scores / row_total).astype(BF)
        attended = jnp.einsum("grs,sd->rgd", attn_probs, value_block, preferred_element_type=F32)
        return (attended, (row_max + jnp.log(row_total))[..., 0])

    def attend_back(packed):
        query_block, key_block, value_block, log_block, grad_block = packed
        scores = masked_scores(query_block, key_block)
        attn_probs = jnp.exp(scores - log_block[..., None])
        grad_value = jnp.einsum(
            "grs,rgd->sd", attn_probs.astype(BF), grad_block, preferred_element_type=F32
        )
        grad_probs = jnp.einsum("rgd,sd->grs", grad_block, value_block, preferred_element_type=F32)
        row_delta = jnp.sum(attn_probs * grad_probs, axis=-1, keepdims=True)
        grad_scores = (attn_probs * (grad_probs - row_delta)).astype(BF)
        grad_query = (
            jnp.einsum("grs,sd->rgd", grad_scores, key_block, preferred_element_type=F32)
            * score_scale
        )
        grad_key = (
            jnp.einsum("grs,rgd->sd", grad_scores, query_block, preferred_element_type=F32)
            * score_scale
        )
        return (grad_query, grad_key, grad_value)

    def forward(layer_input, table):
        cosine_table, sine_table = table
        inverse_one = rms_inverse(layer_input)
        normed_attn = (layer_input * inverse_one * gain_attn).astype(BF)
        qkv = dot_plain(swapped_columns(normed_attn, shard), mat_qkv)
        queries = rotate(
            qkv[:, :query_width].reshape(tok_rows, query_heads, HEAD_DIM), cosine_table, sine_table
        )
        queries = queries.astype(BF).reshape(tok_rows, query_width)
        keys = rotate(
            qkv[:, query_width : query_width + key_width].reshape(tok_rows, key_heads, HEAD_DIM),
            cosine_table,
            sine_table,
        )
        keys = keys.astype(BF).reshape(tok_rows, key_width)
        values = qkv[:, query_width + key_width :].astype(BF)
        pair_all = lax.all_gather(
            jnp.concatenate([keys, values], axis=1), "fsdp", axis=0, tiled=True
        )
        keys_all, values_all = (pair_all[:, :key_width], pair_all[:, key_width:])
        group_out, log_totals = lax.map(attend_group, split_heads(queries, keys_all, values_all))
        attended = group_out.transpose(1, 0, 2, 3).reshape(tok_rows, query_width).astype(BF)
        residual_mid = layer_input + dot_plain(swapped_columns(attended, shard), mat_out)
        inverse_two = rms_inverse(residual_mid)
        normed_mlp = (residual_mid * inverse_two * gain_mlp).astype(BF)
        normed_swapped = swapped_columns(normed_mlp, shard)
        gate_pre = dot_plain(normed_swapped, mat_gate)
        up_proj = dot_plain(normed_swapped, mat_up)
        hidden_act = (jax.nn.silu(gate_pre) * up_proj).astype(BF)
        output = residual_mid + dot_plain(swapped_columns(hidden_act, shard), mat_down)
        return output, (
            layer_input,
            inverse_one,
            normed_attn,
            queries,
            keys_all,
            values_all,
            log_totals,
            attended,
            residual_mid,
            inverse_two,
            normed_mlp,
            gate_pre.astype(BF),
            up_proj.astype(BF),
            hidden_act,
        )

    def backward(grad_top, saved_state, table):
        (
            residual_in,
            inverse_one,
            normed_attn,
            queries,
            keys_all,
            values_all,
            log_totals,
            attended,
            residual_mid,
            inverse_two,
            normed_mlp,
            gate_pre,
            up_proj,
            hidden_act,
        ) = saved_state
        branch_grad = grad_top.astype(BF)
        grad_top = grad_top.astype(F32)
        grad_hidden = swapped_columns(dot_cols(branch_grad, mat_down), shard)
        gate_pre = gate_pre.astype(F32)
        sigmoid_gate = jax.nn.sigmoid(gate_pre)
        grad_gate_pre = (
            grad_hidden
            * up_proj.astype(F32)
            * sigmoid_gate
            * (1.0 + gate_pre * (1.0 - sigmoid_gate))
        ).astype(BF)
        grad_up_proj = (grad_hidden * gate_pre * sigmoid_gate).astype(BF)
        grad_normed = swapped_columns(
            dot_cols(grad_gate_pre, mat_gate) + dot_cols(grad_up_proj, mat_up), shard
        )
        base_mid = residual_mid * inverse_two
        part_gain_mlp = jnp.sum(grad_normed * base_mid, axis=0)
        scaled_grad = grad_normed * gain_mlp
        grad_mid = grad_top + inverse_two * (
            scaled_grad - base_mid * jnp.mean(scaled_grad * base_mid, axis=-1, keepdims=True)
        )
        attn_grad = grad_mid.astype(BF)
        grad_attended = swapped_columns(dot_cols(attn_grad, mat_out).astype(BF), shard)
        query_blocks, key_blocks, value_blocks = split_heads(queries, keys_all, values_all)
        grad_blocks = grad_attended.reshape(tok_rows, key_heads, group_size, HEAD_DIM).transpose(
            1, 0, 2, 3
        )
        grad_queries, grad_keys, grad_values = lax.map(
            attend_back, (query_blocks, key_blocks, value_blocks, log_totals, grad_blocks)
        )
        grad_queries = grad_queries.transpose(1, 0, 2, 3).reshape(tok_rows, query_width)
        grad_keys = grad_keys.transpose(1, 0, 2).reshape(length, key_width)
        grad_values = grad_values.transpose(1, 0, 2).reshape(length, key_width)
        grad_pair = lax.psum_scatter(
            jnp.concatenate([grad_keys, grad_values], axis=1).astype(BF),
            "fsdp",
            scatter_dimension=0,
            tiled=True,
        )
        cosine_table, sine_table = table
        grad_queries = rotate(
            grad_queries.reshape(tok_rows, query_heads, HEAD_DIM), cosine_table, -sine_table
        )
        grad_queries = grad_queries.astype(BF).reshape(tok_rows, query_width)
        grad_keys = rotate(
            grad_pair[:, :key_width].astype(F32).reshape(tok_rows, key_heads, HEAD_DIM),
            cosine_table,
            -sine_table,
        )
        grad_keys = grad_keys.astype(BF).reshape(tok_rows, key_width)
        grad_qkv = jnp.concatenate([grad_queries, grad_keys, grad_pair[:, key_width:]], axis=1)
        grad_normed = swapped_columns(dot_cols(grad_qkv, mat_qkv), shard)
        base_in = residual_in * inverse_one
        part_gain_attn = jnp.sum(grad_normed * base_in, axis=0)
        scaled_grad = grad_normed * gain_attn
        grad_in = grad_mid + inverse_one * (
            scaled_grad - base_in * jnp.mean(scaled_grad * base_in, axis=-1, keepdims=True)
        )
        return (
            grad_in,
            part_gain_attn,
            part_gain_mlp,
            (branch_grad, grad_gate_pre, grad_up_proj, attn_grad, grad_qkv),
        )

    def ahead(x):
        return lax.ppermute(x.astype(BF), "section", [(0, 1)])

    def back(x):
        return lax.ppermute(x.astype(BF), "section", [(1, 0)])

    output, _ = forward(ends_local[0].astype(F32), tables[0])
    received = ahead(output)
    output_one, saved_one = forward(
        jnp.where(first_section, ends_local[1], received).astype(F32), pick(tables[1], tables[0])
    )
    received = ahead(output_one)
    output_two, saved_two = forward(
        jnp.where(first_section, ends_local[0], received).astype(F32), pick(tables[0], tables[1])
    )
    grad_in, _, _, _ = backward(ends_local[0], saved_one, pick(tables[1], tables[0]))
    received = back(grad_in)
    grad_one, gain_attn_one, gain_mlp_one, work_one = backward(
        jnp.where(first_section, received, ends_local[1]), saved_two, pick(tables[0], tables[1])
    )
    received = back(grad_one)
    grad_two, gain_attn_two, gain_mlp_two, work_two = backward(
        jnp.where(first_section, received, ends_local[0]), saved_one, pick(tables[1], tables[0])
    )

    def paired(member):
        own = jnp.concatenate([work_two[member], work_one[member]], axis=0)
        return jnp.concatenate([own, core_swap(own)], axis=0)

    def shares(member):
        x = jnp.concatenate([saved_one[member], saved_two[member]], axis=0)
        width = x.shape[1] // 4
        kept = [column_block(x, shard, width), column_block(x, shard ^ 2, width)]
        given = [
            core_swap(column_block(x, shard ^ 1, width)),
            core_swap(column_block(x, shard ^ 3, width)),
        ]
        return [jnp.concatenate([a, b], axis=0) for a, b in zip(kept, given)]

    chunks = []

    def add_chunks(left, right):
        own_left, other_left = left
        for row in range(0, own_left.shape[1], CHUNK_ROWS):
            for col in range(0, right.shape[1], CHUNK_COLS):
                columns = right[:, col : col + CHUNK_COLS]
                other = dot_rows(other_left[:, row : row + CHUNK_ROWS], columns).astype(BF)
                other = chip_swap(other)
                own = dot_rows(own_left[:, row : row + CHUNK_ROWS], columns)
                chunks.append((own + other.astype(F32)).astype(BF))

    add_chunks(shares(13), paired(0))
    normed = shares(10)
    add_chunks(normed, paired(1))
    add_chunks(normed, paired(2))
    add_chunks(shares(7), paired(3))
    add_chunks(shares(2), paired(4))
    totals = replica_chain(chunks)

    def assembled(rows, cols):
        count = (rows // CHUNK_ROWS) * (cols // CHUNK_COLS)
        taken, totals[:] = totals[:count], totals[count:]
        across = cols // CHUNK_COLS
        lines = [
            jnp.concatenate(taken[at : at + across], axis=1) for at in range(0, count, across)
        ]
        return jnp.concatenate(lines, axis=0).astype(F32)

    grad_down = assembled(w_down.shape[1], w_down.shape[2])
    grad_gate = assembled(w_gate.shape[1], w_gate.shape[2])
    grad_up = assembled(w_up.shape[1], w_up.shape[2])
    grad_out = assembled(w_out.shape[1], w_out.shape[2])
    grad_qkv = assembled(w_query.shape[1], mat_qkv.shape[1])
    gains = jnp.stack([gain_attn_one + gain_attn_two, gain_mlp_one + gain_mlp_two])
    gains = jnp.sum(lax.all_gather(gains, ("fsdp", "dp"), axis=0), axis=0)
    gains = column_block(gains, shard, model_width // 4)
    boundary = jnp.where(
        first_section, jnp.stack([grad_one, grad_two]), jnp.stack([output_one, output_two])
    )
    return (
        boundary[None, :, None],
        gains[0][None],
        grad_qkv[:, :query_width][None],
        grad_qkv[:, query_width : query_width + key_width][None],
        grad_qkv[:, query_width + key_width :][None],
        grad_out[None],
        gains[1][None],
        grad_gate[None],
        grad_up[None],
        grad_down[None],
    )


def solution(mesh):
    return jax.shard_map(
        body,
        mesh=mesh,
        in_specs=(
            P("section", None, "dp", "fsdp", None),
            P(None, "dp", "fsdp"),
            P("section", "fsdp"),
            P("section", "fsdp", None),
            P("section", "fsdp", None),
            P("section", "fsdp", None),
            P("section", "fsdp", None),
            P("section", "fsdp"),
            P("section", "fsdp", None),
            P("section", "fsdp", None),
            P("section", "fsdp", None),
        ),
        out_specs=(
            P("section", None, "dp", "fsdp", None),
            P("section", "fsdp"),
            P("section", "fsdp", None),
            P("section", "fsdp", None),
            P("section", "fsdp", None),
            P("section", "fsdp", None),
            P("section", "fsdp"),
            P("section", "fsdp", None),
            P("section", "fsdp", None),
            P("section", "fsdp", None),
        ),
        check_vma=False,
    )
```

```python
import jax
import jax.numpy as jnp
from jax import lax
from jax.experimental import pallas as pl
from jax.experimental.pallas import tpu as pltpu
from jax.sharding import PartitionSpec as P

HEAD_DIM = 64
GROUP = 4
EPSILON = 1e-05
ROPE_THETA = 500000.0
NEGATIVE = -1e30
LANES = 128
CHUNK_ROWS = 512
CHUNK_COLS = 1024
STREAMS = 2
LEAD = 3
AHEAD = 2
ATTEND_AT = 4
LOWER_AT = 14
VMEM = 56 * 1024 * 1024
BF = jnp.bfloat16
F32 = jnp.float32


def mm(left, right):
    return lax.dot_general(left, right, (((1,), (0,)), ((), ())), preferred_element_type=F32)


def mm_tn(left, right):
    return lax.dot_general(left, right, (((0,), (0,)), ((), ())), preferred_element_type=F32)


def mm_nt(left, right):
    return lax.dot_general(left, right, (((1,), (1,)), ((), ())), preferred_element_type=F32)


def rms_inverse(vector):
    return lax.rsqrt(jnp.mean(vector * vector, axis=-1, keepdims=True) + EPSILON)


def turn(tile, cosine, sine, lane):
    swapped = jnp.where(
        lane % HEAD_DIM < HEAD_DIM // 2,
        pltpu.roll(tile, LANES - HEAD_DIM // 2, axis=1),
        pltpu.roll(tile, HEAD_DIM // 2, axis=1),
    )
    return tile * cosine + swapped * sine


def project_kernel(a_ref, w_ref, cos_ref, sin_ref, q_ref, pair_ref):
    step = pl.program_id(0)
    value = mm(a_ref[...], w_ref[...])
    cosine, sine = cos_ref[...], sin_ref[...]
    lane = lax.broadcasted_iota(jnp.int32, cosine.shape, 1)
    tiles = [value[:, at : at + LANES] for at in range(0, value.shape[1], LANES)]

    @pl.when(step < pl.num_programs(0) - 2)
    def _():
        for index, tile in enumerate(tiles):
            q_ref[:, index * LANES : (index + 1) * LANES] = turn(tile, cosine, sine, lane).astype(BF)

    @pl.when(step >= pl.num_programs(0) - 2)
    def _():
        for index, tile in enumerate(tiles):
            if index % 2 == 0:
                tile = turn(tile, cosine, sine, lane)
            pair_ref[:, index * LANES : (index + 1) * LANES] = tile.astype(BF)


def project(a, weights, cosine, sine, key_width):
    rows, width = a.shape
    total = weights.shape[1]
    tile = key_width
    steps = total // tile
    own = pl.BlockSpec((rows, LANES), lambda t: (0, 0))
    return pl.pallas_call(
        project_kernel,
        grid=(steps,),
        in_specs=[
            pl.BlockSpec((rows, width), lambda t: (0, 0)),
            pl.BlockSpec((width, tile), lambda t: (0, t)),
            own,
            own,
        ],
        out_specs=[
            pl.BlockSpec((rows, tile), lambda t: (0, jnp.minimum(t, steps - 3))),
            pl.BlockSpec((rows, tile), lambda t: (0, jnp.maximum(t - (steps - 2), 0))),
        ],
        out_shape=[
            jax.ShapeDtypeStruct((rows, total - 2 * key_width), BF),
            jax.ShapeDtypeStruct((rows, 2 * key_width), BF),
        ],
        compiler_params=pltpu.CompilerParams(vmem_limit_bytes=VMEM),
        cost_estimate=pl.CostEstimate(flops=1, bytes_accessed=1, transcendentals=0),
    )(a, weights, cosine, sine)


def mm(left, right):
    return lax.dot_general(left, right, (((1,), (0,)), ((), ())), preferred_element_type=F32)


def mm_nt(left, right):
    return lax.dot_general(left, right, (((1,), (1,)), ((), ())), preferred_element_type=F32)


def side_by_side(block):
    turned = block.T
    count = block.shape[1] // HEAD_DIM
    return jnp.concatenate(
        [turned[h * HEAD_DIM : (h + 1) * HEAD_DIM] for h in range(count)], axis=1
    )


def stacked(block):
    count = block.shape[1] // HEAD_DIM
    return jnp.concatenate(
        [block[:, h * HEAD_DIM : (h + 1) * HEAD_DIM] for h in range(count)], axis=0
    )


def causal_scores(keys, queries_t, rows, blocks):
    scores = mm(keys, queries_t)
    tail = scores[(blocks - 1) * rows :]
    key_at = lax.broadcasted_iota(jnp.int32, tail.shape, 0)
    query_at = lax.broadcasted_iota(jnp.int32, tail.shape, 1) % rows
    tail = jnp.where(key_at <= query_at, tail, NEGATIVE)
    if blocks == 1:
        return tail
    return jnp.concatenate([scores[: (blocks - 1) * rows], tail], axis=0)


def attend_kernel(shard_ref, q_ref, kv_ref, o_ref, lse_ref):
    rows = q_ref.shape[0]
    span = GROUP * HEAD_DIM
    pair = 2 * HEAD_DIM
    for blocks in range(1, kv_ref.shape[0] // rows + 1):

        @pl.when(shard_ref[0] == blocks - 1)
        def _():
            for half in range(2):
                at = half * HEAD_DIM
                queries = q_ref[:, half * span : (half + 1) * span]
                keys = kv_ref[: blocks * rows, at : at + HEAD_DIM]
                values = kv_ref[: blocks * rows, pair + at : pair + at + HEAD_DIM]
                queries_t = side_by_side(queries) * jnp.asarray(HEAD_DIM**-0.5, BF)
                scores = causal_scores(keys, queries_t, rows, blocks)
                top = jnp.max(scores, axis=0, keepdims=True)
                weights = jnp.exp(scores - top)
                total = jnp.sum(weights, axis=0, keepdims=True)
                out_t = mm(values.T, weights.astype(BF)) / total
                out_t = jnp.concatenate(
                    [out_t[:, h * rows : (h + 1) * rows] for h in range(GROUP)], axis=0
                )
                o_ref[:, half * span : (half + 1) * span] = out_t.T.astype(BF)
                lse_ref[0, half : half + 1, :] = top + jnp.log(total)


def attend(shard, queries, pairs):
    rows, width = queries.shape
    length, pair_width = pairs.shape
    steps = pair_width // (4 * HEAD_DIM)
    span = 2 * GROUP * HEAD_DIM
    return pl.pallas_call(
        attend_kernel,
        grid_spec=pltpu.PrefetchScalarGridSpec(
            num_scalar_prefetch=1,
            grid=(steps,),
            in_specs=[
                pl.BlockSpec((rows, span), lambda p, s: (0, p)),
                pl.BlockSpec((length, 4 * HEAD_DIM), lambda p, s: (0, p)),
            ],
            out_specs=[
                pl.BlockSpec((rows, span), lambda p, s: (0, p)),
                pl.BlockSpec((1, 2, GROUP * rows), lambda p, s: (p, 0, 0)),
            ],
        ),
        out_shape=[
            jax.ShapeDtypeStruct((rows, width), BF),
            jax.ShapeDtypeStruct((steps, 2, GROUP * rows), F32),
        ],
        compiler_params=pltpu.CompilerParams(vmem_limit_bytes=VMEM),
        cost_estimate=pl.CostEstimate(flops=1, bytes_accessed=1, transcendentals=0),
    )(shard, queries, pairs)


def attend_back_kernel(
    shard_ref, q_ref, kv_ref, lse_ref, do_ref, cos_ref, sin_ref, kcos_ref, ksin_ref, dq_ref, dkv_ref
):
    rows = q_ref.shape[0]
    span = GROUP * HEAD_DIM
    pair = 2 * HEAD_DIM
    wide = HEAD_DIM // 2
    scale = HEAD_DIM**-0.5
    for blocks in range(1, kv_ref.shape[0] // rows + 1):

        @pl.when(shard_ref[0] == blocks - 1)
        def _():
            seen = blocks * rows
            key_grads = []
            for half in range(2):
                at = half * HEAD_DIM
                queries = q_ref[:, half * span : (half + 1) * span]
                grads = do_ref[:, half * span : (half + 1) * span]
                keys = kv_ref[:seen, at : at + HEAD_DIM]
                values = kv_ref[:seen, pair + at : pair + at + HEAD_DIM]
                queries_t = side_by_side(queries) * jnp.asarray(scale, BF)
                grads_t = side_by_side(grads)
                scores = causal_scores(keys, queries_t, rows, blocks)
                weights = jnp.exp(scores - lse_ref[0, half : half + 1, :])
                moved = mm(values, grads_t)
                product = weights * moved
                delta = jnp.sum(product, axis=0, keepdims=True)
                grad_scores = (product - weights * delta).astype(BF)
                dkv_ref[:seen, pair + at : pair + at + HEAD_DIM] = mm(
                    weights.astype(BF), stacked(grads)
                ).astype(BF)
                key_grads.append(mm(grad_scores, stacked(queries)) * scale)
                grad_t = mm(keys.T, grad_scores) * scale
                turned = []
                for h in range(GROUP):
                    block = grad_t[:, h * rows : (h + 1) * rows]
                    first, second = block[:wide], block[wide:]
                    turned.append(first * cos_ref[...] + second * sin_ref[...])
                    turned.append(second * cos_ref[...] - first * sin_ref[...])
                dq_ref[:, half * span : (half + 1) * span] = (
                    jnp.concatenate(turned, axis=0).T.astype(BF)
                )
            key_grads = jnp.concatenate(key_grads, axis=1)
            lane = lax.broadcasted_iota(jnp.int32, key_grads.shape, 1)
            dkv_ref[:seen, :pair] = turn(
                key_grads, kcos_ref[:seen, :], -ksin_ref[:seen, :], lane
            ).astype(BF)
            if seen < kv_ref.shape[0]:
                dkv_ref[seen:, :] = jnp.zeros((kv_ref.shape[0] - seen, 2 * pair), BF)


def attend_back(shard, queries, pairs, lse, grads, cosine, sine, key_cosine, key_sine):
    rows, width = queries.shape
    length, pair_width = pairs.shape
    steps = pair_width // (4 * HEAD_DIM)
    span = 2 * GROUP * HEAD_DIM
    table = pl.BlockSpec((HEAD_DIM // 2, rows), lambda p, s: (0, 0))
    key_table = pl.BlockSpec((length, LANES), lambda p, s: (0, 0))
    return pl.pallas_call(
        attend_back_kernel,
        grid_spec=pltpu.PrefetchScalarGridSpec(
            num_scalar_prefetch=1,
            grid=(steps,),
            in_specs=[
                pl.BlockSpec((rows, span), lambda p, s: (0, p)),
                pl.BlockSpec((length, 4 * HEAD_DIM), lambda p, s: (0, p)),
                pl.BlockSpec((1, 2, GROUP * rows), lambda p, s: (p, 0, 0)),
                pl.BlockSpec((rows, span), lambda p, s: (0, p)),
                table,
                table,
                key_table,
                key_table,
            ],
            out_specs=[
                pl.BlockSpec((rows, span), lambda p, s: (0, p)),
                pl.BlockSpec((length, 4 * HEAD_DIM), lambda p, s: (0, p)),
            ],
        ),
        out_shape=[
            jax.ShapeDtypeStruct((rows, width), BF),
            jax.ShapeDtypeStruct((length, pair_width), BF),
        ],
        compiler_params=pltpu.CompilerParams(vmem_limit_bytes=VMEM),
        cost_estimate=pl.CostEstimate(flops=1, bytes_accessed=1, transcendentals=0),
    )(shard, queries, pairs, lse, grads, cosine, sine, key_cosine, key_sine)


def widen_kernel(shard_ref, b_ref, *refs):
    gates, ups = refs[:4], refs[4:8]
    z_ref, g_ref, u_ref = refs[8:]
    depth = gates[0].shape[0]
    gate = up = None
    for k in range(4):
        at = pl.multiple_of((shard_ref[0] ^ k) * depth, depth)
        left = b_ref[:, pl.ds(at, depth)]
        g, u = mm(left, gates[k][...]), mm(left, ups[k][...])
        gate, up = (g, u) if gate is None else (gate + g, up + u)
    z_ref[...] = (gate * jax.nn.sigmoid(gate) * up).astype(BF)
    g_ref[...] = gate.astype(BF)
    u_ref[...] = up.astype(BF)


def widen(shard, b, gates, ups, tile=512):
    rows, width = b.shape
    depth, hidden = gates[0].shape
    out = pl.BlockSpec((rows, tile), lambda t, s: (0, t))
    return pl.pallas_call(
        widen_kernel,
        grid_spec=pltpu.PrefetchScalarGridSpec(
            num_scalar_prefetch=1,
            grid=(hidden // tile,),
            in_specs=[pl.BlockSpec((rows, width), lambda t, s: (0, 0))]
            + [pl.BlockSpec((depth, tile), lambda t, s: (0, t))] * 8,
            out_specs=[out] * 3,
        ),
        out_shape=[jax.ShapeDtypeStruct((rows, hidden), BF)] * 3,
        compiler_params=pltpu.CompilerParams(vmem_limit_bytes=VMEM),
        cost_estimate=pl.CostEstimate(flops=1, bytes_accessed=1, transcendentals=0),
    )(shard, b, *gates, *ups)


def narrow_kernel(shard_ref, z_ref, m_ref, *refs):
    lows, highs, y_ref = refs[:4], refs[4:8], refs[8]
    step = pl.program_id(0)
    depth = lows[0].shape[0]

    def one(downs):
        total = m_ref[...]
        for k in range(4):
            at = pl.multiple_of((shard_ref[0] ^ k) * depth, depth)
            total = total + mm(z_ref[:, pl.ds(at, depth)], downs[k][...])
        y_ref[...] = total

    @pl.when(step < pl.num_programs(0) // 2)
    def _():
        one(lows)

    @pl.when(step >= pl.num_programs(0) // 2)
    def _():
        one(highs)


def narrow(shard, z, m, lows, highs, tile=256):
    rows, hidden = z.shape
    depth, half = lows[0].shape
    width = 2 * half
    per = half // tile
    block = pl.BlockSpec((rows, tile), lambda t, s: (0, t))
    low = pl.BlockSpec((depth, tile), lambda t, s: (0, jnp.minimum(t, per - 1)))
    high = pl.BlockSpec((depth, tile), lambda t, s: (0, jnp.maximum(t - per, 0)))
    return pl.pallas_call(
        narrow_kernel,
        grid_spec=pltpu.PrefetchScalarGridSpec(
            num_scalar_prefetch=1,
            grid=(2 * per,),
            in_specs=[pl.BlockSpec((rows, hidden), lambda t, s: (0, 0)), block]
            + [low] * 4
            + [high] * 4,
            out_specs=block,
        ),
        out_shape=jax.ShapeDtypeStruct((rows, width), F32),
        compiler_params=pltpu.CompilerParams(vmem_limit_bytes=VMEM),
        cost_estimate=pl.CostEstimate(flops=1, bytes_accessed=1, transcendentals=0),
    )(shard, z, m, *lows, *highs)


def hidden_back_kernel(shard_ref, dy_ref, g_ref, u_ref, *refs):
    lows, highs, gates, ups = refs[:4], refs[4:8], refs[8:12], refs[12:16]
    dg_ref, du_ref, db_ref, total = refs[16:]
    middle = lows[0].shape[1]
    step = pl.program_id(0)
    per = pl.num_programs(0) // 4
    depth = gates[0].shape[0]

    def one(low, high):
        dz = mm_nt(dy_ref[:, :middle], low[...]) + mm_nt(dy_ref[:, middle:], high[...])
        gate = g_ref[...].astype(F32)
        up = u_ref[...].astype(F32)
        slope = jax.nn.sigmoid(gate)
        dg = (dz * up * slope * (1.0 + gate * (1.0 - slope))).astype(BF)
        du = (dz * gate * slope).astype(BF)
        dg_ref[...] = dg
        du_ref[...] = du
        for k in range(4):
            part = mm_nt(dg, gates[k][...]) + mm_nt(du, ups[k][...])
            at = pl.multiple_of((shard_ref[0] ^ k) * depth, depth)

            @pl.when(step == 0)
            def _():
                total[:, pl.ds(at, depth)] = part

            @pl.when(step > 0)
            def _():
                total[:, pl.ds(at, depth)] += part

    for k in range(4):

        @pl.when(step // per == k)
        def _():
            one(lows[k], highs[k])

    @pl.when(step == pl.num_programs(0) - 1)
    def _():
        db_ref[...] = total[...]


def hidden_back(shard, dy, g, u, lows, highs, gates, ups, tile=512):
    rows, width = dy.shape
    hidden = g.shape[1]
    depth = gates[0].shape[0]
    per = hidden // 4 // tile

    def natural(t, s):
        return (0, (s[0] ^ (t // per)) * per + t % per)

    def piece(k):
        return lambda t, s: (jnp.clip(t - k * per, 0, per - 1), 0)

    cols = pl.BlockSpec((rows, tile), natural)
    whole = pl.BlockSpec((rows, width), lambda t, s: (0, 0))
    return pl.pallas_call(
        hidden_back_kernel,
        grid_spec=pltpu.PrefetchScalarGridSpec(
            num_scalar_prefetch=1,
            grid=(hidden // tile,),
            in_specs=[whole, cols, cols]
            + [pl.BlockSpec((tile, width // 2), piece(k)) for k in (0, 1, 2, 3, 0, 1, 2, 3)]
            + [pl.BlockSpec((depth, tile), natural)] * 8,
            out_specs=[cols, cols, whole],
            scratch_shapes=[pltpu.VMEM((rows, width), F32)],
        ),
        out_shape=[
            jax.ShapeDtypeStruct((rows, hidden), BF),
            jax.ShapeDtypeStruct((rows, hidden), BF),
            jax.ShapeDtypeStruct((rows, width), F32),
        ],
        compiler_params=pltpu.CompilerParams(vmem_limit_bytes=VMEM),
        cost_estimate=pl.CostEstimate(flops=1, bytes_accessed=1, transcendentals=0),
    )(shard, dy, g, u, *lows, *highs, *gates, *ups)


def outer(x, row, parts, column, width, added=None, earlier=None, tile=512):
    per = (CHUNK_COLS if added is not None else width) // tile
    count = width // tile // per
    first = column // tile
    at = row // CHUNK_ROWS
    held = [] if added is None else [added]
    extra = [] if earlier is None else [earlier]

    def kernel(*refs):
        step = pl.program_id(0)
        left = jnp.concatenate([part[...] for part in refs[: len(x)]], axis=1)
        refs = refs[len(x) :]
        right = jnp.concatenate([part[...] for part in refs[: len(parts)]], axis=0)
        value = mm(left, right)
        if held:
            value = value + refs[len(parts)][...].astype(F32)
        for index in range(count):

            @pl.when(step // per == index)
            def _():
                refs[len(parts) + len(held) + len(extra) + index][...] = value.astype(BF)

    def chunk(index):
        return lambda t: (0, jnp.clip(t - index * per, 0, per - 1))

    return pl.pallas_call(
        kernel,
        grid=(count * per,),
        in_specs=[pl.BlockSpec((CHUNK_ROWS, part.shape[1]), lambda t: (at, 0)) for part in x]
        + [pl.BlockSpec((part.shape[0], tile), lambda t: (0, first + t)) for part in parts]
        + [pl.BlockSpec((CHUNK_ROWS, tile), lambda t: (0, t))] * len(held)
        + [pl.BlockSpec(memory_space=pl.ANY)] * len(extra),
        out_specs=[pl.BlockSpec((CHUNK_ROWS, tile), chunk(index)) for index in range(count)],
        out_shape=[jax.ShapeDtypeStruct((CHUNK_ROWS, per * tile), BF)] * count,
        compiler_params=pltpu.CompilerParams(vmem_limit_bytes=VMEM),
        cost_estimate=pl.CostEstimate(flops=1, bytes_accessed=1, transcendentals=0),
    )(*x, *parts, *held, *extra)


def core_swap(x):
    return lax.ppermute(x, "fsdp", [(0, 1), (1, 0), (2, 3), (3, 2)])


def chip_swap(x):
    return lax.ppermute(x, "fsdp", [(0, 2), (2, 0), (1, 3), (3, 1)])


def after(value, other):
    always = lax.axis_index("dp") > -7
    return jnp.where(always, value, other.reshape(-1)[0].astype(value.dtype))


def nothing_kernel(*refs):
    pass


def hold(x, *others):
    anywhere = pl.BlockSpec(memory_space=pl.ANY)
    return pl.pallas_call(
        nothing_kernel,
        in_specs=[anywhere] * (1 + len(others)),
        out_specs=anywhere,
        out_shape=jax.ShapeDtypeStruct(x.shape, x.dtype),
        input_output_aliases={0: 0},
        compiler_params=pltpu.CompilerParams(vmem_limit_bytes=VMEM),
        cost_estimate=pl.CostEstimate(flops=1, bytes_accessed=1, transcendentals=0),
    )(x, *others)


def turned_kernel(shard_ref, *refs):
    for k in range(4):
        refs[4 + k][...] = refs[k][...].T


def turned_blocks(shard, x, tile=512):
    rows, width = x.shape
    per = width // 4 // tile

    def block(k):
        return pl.BlockSpec((rows, tile), lambda t, s: (0, (s[0] ^ k) * per + t))

    return pl.pallas_call(
        turned_kernel,
        grid_spec=pltpu.PrefetchScalarGridSpec(
            num_scalar_prefetch=1,
            grid=(per,),
            in_specs=[block(k) for k in range(4)],
            out_specs=[pl.BlockSpec((tile, rows), lambda t, s: (t, 0))] * 4,
        ),
        out_shape=[jax.ShapeDtypeStruct((width // 4, rows), x.dtype)] * 4,
        compiler_params=pltpu.CompilerParams(vmem_limit_bytes=VMEM),
        cost_estimate=pl.CostEstimate(flops=1, bytes_accessed=1, transcendentals=0),
    )(shard, x, x, x, x)


def column_block(x, index, width):
    return lax.dynamic_slice_in_dim(x, index * width, width, axis=1)


def relay_kernel(names, places, root, place_ref, *refs):
    named = dict(zip(names, refs))
    up_ref, down_ref = refs[-2:]
    place = place_ref[0]

    def read(name):
        return named[name][...].astype(F32) if name in named else 0.0

    own = 0.0
    for name, held_by in places:
        if name not in named:
            continue
        mine = held_by[0] == place
        for position in held_by[1:]:
            mine = mine | (place == position)
        own = jnp.where(mine, named[name][...].astype(F32), own)
    total = own + read("below_held") + read("above_held")
    up = jnp.where(place == root, total, read("below") + jnp.where(place < root, own, 0.0))
    down = jnp.where(place == root, total, read("above") + jnp.where(place > root, own, 0.0))
    up_ref[...] = jnp.broadcast_to(up, up_ref.shape).astype(up_ref.dtype)
    down_ref[...] = jnp.broadcast_to(down, down_ref.shape).astype(down_ref.dtype)


def relay(place, root, places, operands, earlier, shape, kind):
    names = [name for name in operands if operands[name] is not None]
    unique, at = [], {}
    for name in names:
        for index, other in enumerate(unique):
            if operands[name] is other:
                at[name] = index
        if name not in at:
            at[name] = len(unique)
            unique.append(operands[name])
    rows, cols = shape
    tile = rows // 2 if rows >= 256 else rows
    block = pl.BlockSpec((tile, cols), lambda t, s: (t, 0))

    def kernel(place_ref, *refs):
        values = refs[: len(unique)]
        relay_kernel(names, places, root, place_ref, *[values[at[n]] for n in names], *refs[-2:])

    return pl.pallas_call(
        kernel,
        grid_spec=pltpu.PrefetchScalarGridSpec(
            num_scalar_prefetch=1,
            grid=(rows // tile,),
            in_specs=[block] * len(unique) + [pl.BlockSpec(memory_space=pl.ANY)] * len(earlier),
            out_specs=[block, block],
        ),
        out_shape=[jax.ShapeDtypeStruct(shape, kind)] * 2,
        compiler_params=pltpu.CompilerParams(vmem_limit_bytes=VMEM),
        cost_estimate=pl.CostEstimate(flops=1, bytes_accessed=1, transcendentals=0),
    )(place, *unique, *earlier)


def replica_chain(count, make, shape, kind, stream_count=STREAMS, wanted=None):
    peers = lax.axis_size("dp")
    place = lax.axis_index("dp")
    place_vector = place.astype(jnp.int32).reshape(1)
    root = (peers - 1) // 2
    delay = max(root, peers - 1 - root)
    up_pairs = [(i, i + 1) for i in range(peers - 1)]
    down_pairs = [(i + 1, i) for i in range(peers - 1)]
    counts = [len(range(q, count, stream_count)) for q in range(stream_count)]
    streams = [[] for _ in counts]
    ups = [[] for _ in streams]
    downs = [[] for _ in streams]
    sent = [[] for _ in streams]
    order = []
    lags = [
        position if position < root else delay if position == root else peers - 1 - position
        for position in range(peers)
    ]

    def nth(items, index):
        return items[index] if 0 <= index < len(items) else None

    for step in range(max(counts) + 2 * delay):
        for q in range(stream_count):
            if step >= counts[q] + 2 * delay:
                continue
            if wanted is not None and order:
                wanted(len(order), order[-1][0])
            if step < counts[q]:
                before = order[-LEAD][0] if len(order) >= LEAD else None
                streams[q].append(make(q + step * stream_count, before))
            places, operands = [], {}
            for lag in sorted(set(lags)):
                name = f"own{lag}"
                operands[name] = nth(streams[q], step - lag)
                places.append((name, [p for p in range(peers) if lags[p] == lag]))
            operands["below"] = nth(ups[q], step - 1)
            operands["above"] = nth(downs[q], step - 1)
            operands["below_held"] = nth(ups[q], step - 1 - (delay - root))
            operands["above_held"] = nth(downs[q], step - 1 - (delay - (peers - 1 - root)))
            earlier = ()
            if stream_count > 1 and len(order) > stream_count:
                earlier = order[-(stream_count + 1)]
            up, down = relay(place_vector, root, places, operands, earlier, shape, kind)
            sent[q].append((up, down))
            if step < counts[q] + 2 * delay - 1:
                ups[q].append(lax.ppermute(up, "dp", up_pairs))
                downs[q].append(lax.ppermute(down, "dp", down_pairs))
                order.append((ups[q][-1], downs[q][-1]))
    distance = jnp.abs(place - root)
    totals = [None] * count
    for q in range(stream_count):
        for index in range(counts[q]):
            total = None
            for hops in range(delay + 1):
                up, down = sent[q][index + delay + hops]
                value = jnp.where(place >= root, up, down)
                total = value if total is None else jnp.where(distance == hops, value, total)
            totals[q + index * stream_count] = total
    return totals


def body(
    ends, positions, attn_gain, w_query, w_key, w_value, w_out, mlp_gain, w_gate, w_up, w_down
):
    shard = lax.axis_index("fsdp")
    shard_vector = shard.astype(jnp.int32).reshape(1)
    replica = lax.axis_index("dp")
    replicas = lax.axis_size("dp")
    first_section = lax.axis_index("section") == 0
    tok_rows = ends.shape[3]
    model_width = ends.shape[4]
    length = tok_rows * lax.axis_size("fsdp")
    key_width = w_key.shape[2]
    query_width = w_query.shape[2]
    ends_local = ends[0, :, 0]

    gains = lax.all_gather(
        jnp.concatenate([attn_gain, mlp_gain], axis=0), "fsdp", axis=1, tiled=True
    ).astype(F32)
    gain_attn, gain_mlp = gains[0], gains[1]
    places_all = lax.all_gather(positions[:, 0], "fsdp", axis=1, tiled=True)
    start = gain_attn[0] + places_all[0, 0].astype(F32)

    def rotary(micro_first, micro_second):
        places = jnp.where(first_section, places_all[micro_first], places_all[micro_second])
        half = HEAD_DIM // 2
        frequency = jnp.exp(-jnp.log(ROPE_THETA) * 2.0 * jnp.arange(half, dtype=F32) / HEAD_DIM)
        angles = places.astype(F32)[:, None] * frequency[None, :]
        cosine, sine = jnp.cos(angles), jnp.sin(angles)
        own = [lax.dynamic_slice_in_dim(x, shard * tok_rows, tok_rows, 0) for x in (cosine, sine)]
        lanes = LANES // HEAD_DIM
        wide = (
            jnp.tile(cosine, (1, 2 * lanes)),
            jnp.tile(jnp.concatenate([-sine, sine], axis=1), (1, lanes)),
        )
        wide_own = [lax.dynamic_slice_in_dim(x, shard * tok_rows, tok_rows, 0) for x in wide]
        return wide_own, (own[0].T, own[1].T), wide

    table_a = rotary(1, 0)
    table_b = rotary(0, 1)

    def part(x):
        rows = x.shape[0] // replicas
        return lax.dynamic_slice_in_dim(x, replica * rows, rows, axis=0)

    def spread(x):
        return lax.all_gather(x, "dp", axis=0, tiled=True)

    pieces = [w_query[0]]
    for at in range(0, key_width, LANES):
        pieces += [w_key[0, :, at : at + LANES], w_value[0, :, at : at + LANES]]
    own_qkv = jnp.concatenate(pieces, axis=1)
    own_out, own_gate, own_up, own_down = w_out[0], w_gate[0], w_up[0], w_down[0]
    middle = own_gate.shape[1] // 2
    sends = [part(own_gate[:, :middle]), part(own_gate[:, middle:])]
    sends += [part(own_out), own_qkv, part(own_up)]
    got = []
    spreads = []
    for index, send in enumerate(sends):
        send = after(send, (start, *got)[(0, 1, 2, 2, 3)[index]])
        if index == 4:
            send = after(send, spreads[0])
        got.append(chip_swap(send))
        if index != 3:
            spreads.append(spread(got[-1]))
    half = own_down.shape[1] // 2
    other_low = chip_swap(after(own_down[:, :half], got[3]))

    def shards(own, other):
        return (own, core_swap(own), other, core_swap(other))

    def natural(values):
        rows = values[0].shape[0]
        whole = jnp.zeros((4 * rows, values[0].shape[1]), BF)
        for k, value in enumerate(values):
            whole = lax.dynamic_update_slice(whole, value, ((shard ^ k) * rows, 0))
        return whole

    gates = shards(own_gate, jnp.concatenate(spreads[:2], axis=1))
    mat_qkv = natural(shards(own_qkv, got[3]))
    mat_out = natural(shards(own_out, spreads[2]))

    def all_rows(x):
        return shards(x, chip_swap(x))

    def summed_rows(x):
        def rows_of(index):
            return lax.dynamic_slice_in_dim(x, index * tok_rows, tok_rows, 0)

        near = rows_of(shard).astype(F32) + core_swap(rows_of(shard ^ 1)).astype(F32)
        far = rows_of(shard ^ 2).astype(F32) + core_swap(rows_of(shard ^ 3)).astype(F32)
        return (near + chip_swap(far.astype(BF)).astype(F32)).astype(BF)

    def enter(layer_input, table):
        inverse_one = rms_inverse(layer_input)
        normed_attn = (layer_input * inverse_one * gain_attn).astype(BF)
        queries, pairs = project(normed_attn, mat_qkv, *table[0], key_width)
        return inverse_one, normed_attn, queries, natural(all_rows(pairs))

    def middle_part(layer_input, entered, *waits):
        held = shard_vector
        for other in waits:
            held = after(held, other)
        attended, log_totals = attend(held, entered[2], entered[3])
        residual_mid = layer_input + mm(attended, mat_out)
        inverse_two = rms_inverse(residual_mid)
        normed_mlp = (residual_mid * inverse_two * gain_mlp).astype(BF)
        return attended, log_totals, residual_mid, inverse_two, normed_mlp

    def leave(layer_input, entered, halfway):
        inverse_one, normed_attn, queries, pairs_all = entered
        attended, log_totals, residual_mid, inverse_two, normed_mlp = halfway
        hidden_act, gate_pre, up_proj = widen(shard_vector, normed_mlp, gates, ups)
        output = narrow(shard_vector, hidden_act, residual_mid, lows, highs)
        return output, {
            "input": layer_input,
            "inverse_one": inverse_one,
            "a": normed_attn,
            "queries": queries,
            "pairs": pairs_all,
            "log": log_totals,
            "o": attended,
            "mid": residual_mid,
            "inverse_two": inverse_two,
            "b": normed_mlp,
            "gate": gate_pre,
            "up": up_proj,
            "z": hidden_act,
        }

    def back_upper(grad_top, saved):
        grad_gate_pre, grad_up_proj, grad_normed = hidden_back(
            shard_vector, grad_top, saved["gate"], saved["up"], lows, highs, gates, ups
        )
        inverse_two = saved["inverse_two"]
        base_mid = saved["mid"] * inverse_two
        part_gain_mlp = jnp.sum(grad_normed * base_mid, axis=0)
        scaled_grad = grad_normed * gain_mlp
        grad_mid = grad_top.astype(F32) + inverse_two * (
            scaled_grad - base_mid * jnp.mean(scaled_grad * base_mid, axis=-1, keepdims=True)
        )
        attn_grad = grad_mid.astype(BF)
        return grad_gate_pre, grad_up_proj, attn_grad, grad_mid, part_gain_mlp

    def back_attention(upper, saved, table, *waits):
        held = shard_vector
        for other in waits:
            held = after(held, other)
        grad_attended = mm_nt(upper[2], mat_out).astype(BF)
        grad_queries, grad_pairs = attend_back(
            held, saved["queries"], saved["pairs"], saved["log"], grad_attended, *table[1], *table[2]
        )

        def rows_of(index):
            return lax.dynamic_slice_in_dim(grad_pairs, index * tok_rows, tok_rows, 0)

        far = rows_of(shard ^ 2).astype(F32) + core_swap(rows_of(shard ^ 3)).astype(F32)
        far = chip_swap(far.astype(BF))
        near = rows_of(shard).astype(F32) + core_swap(rows_of(shard ^ 1)).astype(F32)
        return grad_queries, near, far

    def back_lower(upper, attention, saved, *waits):
        grad_queries, near, far = attention
        if waits:
            far = hold(far, *waits)
        grad_qkv = jnp.concatenate([grad_queries, (near + far.astype(F32)).astype(BF)], axis=1)
        grad_normed = mm_nt(grad_qkv, mat_qkv)
        base_in = saved["input"] * saved["inverse_one"]
        part_gain_attn = jnp.sum(grad_normed * base_in, axis=0)
        scaled_grad = grad_normed * gain_attn
        grad_in = upper[3] + saved["inverse_one"] * (
            scaled_grad - base_in * jnp.mean(scaled_grad * base_in, axis=-1, keepdims=True)
        )
        return grad_in, grad_qkv, jnp.stack([part_gain_attn, upper[4]])

    def ahead(x):
        return lax.ppermute(x.astype(BF), "section", [(0, 1)])

    def back(x):
        return lax.ppermute(x.astype(BF), "section", [(1, 0)])

    def choose(first, second):
        return jnp.where(first_section, first, second)

    layer_input = ends_local[0].astype(F32)
    entered = enter(layer_input, table_b)
    other_high = chip_swap(after(own_down[:, half:], entered[3]))
    halfway = middle_part(layer_input, entered)
    lows = shards(own_down[:, :half], hold(other_low, halfway[4]))
    ups = shards(own_up, hold(spreads[3], halfway[4], lows[2]))
    highs = shards(own_down[:, half:], hold(other_high, ups[2]))
    output, _ = leave(layer_input, entered, halfway)
    received = ahead(output)
    layer_input = choose(ends_local[1], received).astype(F32)
    entered = enter(layer_input, table_a)
    output_one, saved_a = leave(layer_input, entered, middle_part(layer_input, entered))
    received = ahead(output_one)
    turned_a = turned_blocks(shard_vector, saved_a["z"])
    layer_input = choose(ends_local[0], received).astype(F32)
    entered = enter(layer_input, table_b)
    halfway = middle_part(layer_input, entered, turned_a[0])
    output_two, saved_b = leave(layer_input, entered, halfway)
    turned_b = turned_blocks(shard_vector, saved_b["z"])

    def shares(blocks_a, blocks_b):
        near = (blocks_a[0], blocks_b[0], core_swap(blocks_a[1]), core_swap(blocks_b[1]))
        far = (blocks_a[2], blocks_b[2], core_swap(blocks_a[3]), core_swap(blocks_b[3]))
        return near, far

    def shares_of(name):
        return shares(
            turned_blocks(shard_vector, saved_a[name]), turned_blocks(shard_vector, saved_b[name])
        )

    def chip_rows(first, second):
        return (first, second, core_swap(first), core_swap(second))

    upper = back_upper(ends_local[0], saved_a)
    grad_in, _, _ = back_lower(upper, back_attention(upper, saved_a, table_a), saved_a)
    received = back(grad_in)
    top_b = choose(received, ends_local[1])
    upper_b = back_upper(top_b, saved_b)
    attention = back_attention(upper_b, saved_b, table_b)
    grad_one, grad_qkv_b, gains_b = back_lower(upper_b, attention, saved_b, turned_b[0])
    received = back(grad_one)
    top_a = choose(received, ends_local[0])

    late = {"down": (shares(turned_a, turned_b), chip_rows(top_a, top_b))}
    work = {}

    def begin_last(begun):
        work["upper"] = upper_a = back_upper(after(top_a, begun), saved_a)
        normed = shares_of("b")
        late["gate"] = (normed, chip_rows(upper_a[0], upper_b[0]))
        late["up"] = (normed, chip_rows(upper_a[1], upper_b[1]))
        late["out"] = (shares_of("o"), chip_rows(upper_a[2], upper_b[2]))

    def wanted(sends, last):
        if sends == ATTEND_AT:
            work["attention"] = back_attention(work["upper"], saved_a, table_a, last)
        if sends == LOWER_AT:
            work["done"] = back_lower(work["upper"], work["attention"], saved_a, last)
            late["attn"] = (shares_of("a"), chip_rows(work["done"][1], grad_qkv_b))

    pair = 2 * CHUNK_COLS
    hidden_width = w_gate.shape[2]
    qkv_width = query_width + 2 * key_width
    plan = []
    for row in range(0, w_down.shape[1], CHUNK_ROWS):
        plan += [("down", row, col, pair) for col in range(0, model_width, pair)]
    for name, width in (("gate", hidden_width), ("up", hidden_width), ("out", model_width)):
        plan += [(name, 0, col, pair) for col in range(0, width, pair)]
    plan += [("attn", 0, col, min(pair, qkv_width - col)) for col in range(0, qkv_width, pair)]
    crossed = []
    made = []

    def cross(earlier):
        name, row, col, width = plan[len(crossed)]
        (own, other), parts = late[name]
        (result,) = outer(other, row, parts, col, width, None, earlier)
        crossed.append(chip_swap(result))
        return result

    def make(index, earlier):
        if index == len(made):
            at = index // 2
            ahead_to = min(at + (AHEAD if at > 0 else 1), len(plan) - 1)
            while len(crossed) <= ahead_to and plan[len(crossed)][0] in late:
                result = cross(earlier)
            if index == 0:
                begin_last(result)
                earlier = work["upper"][0]
            name, row, col, width = plan[at]
            (own, other), parts = late[name]
            made.extend(outer(own, row, parts, col, width, crossed[at], earlier))
        return made[index]

    count = sum(width // CHUNK_COLS for _, _, _, width in plan)
    totals = replica_chain(count, make, (CHUNK_ROWS, CHUNK_COLS), BF, wanted=wanted)
    grad_two, _, gains_a = work["done"]

    gains = gains_a + gains_b
    gains = gains + core_swap(gains)
    gains = gains + chip_swap(gains)
    gains = column_block(gains, shard, model_width // 4)
    (gains,) = replica_chain(1, lambda index, earlier: gains, gains.shape, F32, 1)

    def assembled(rows, cols):
        count = (rows // CHUNK_ROWS) * (cols // CHUNK_COLS)
        taken, totals[:] = totals[:count], totals[count:]
        across = cols // CHUNK_COLS
        lines = [
            jnp.concatenate(taken[at : at + across], axis=1) for at in range(0, count, across)
        ]
        return jnp.concatenate(lines, axis=0).astype(F32)

    grad_down = assembled(w_down.shape[1], w_down.shape[2])
    grad_gate = assembled(w_gate.shape[1], w_gate.shape[2])
    grad_up = assembled(w_up.shape[1], w_up.shape[2])
    grad_out = assembled(w_out.shape[1], w_out.shape[2])
    grad_qkv = assembled(w_query.shape[1], mat_qkv.shape[1])
    grad_pairs = [
        grad_qkv[:, at : at + LANES] for at in range(query_width, grad_qkv.shape[1], LANES)
    ]
    boundary = choose(jnp.stack([grad_one, grad_two]), jnp.stack([output_one, output_two]))
    return (
        boundary[None, :, None],
        gains[0][None],
        grad_qkv[:, :query_width][None],
        jnp.concatenate(grad_pairs[::2], axis=1)[None],
        jnp.concatenate(grad_pairs[1::2], axis=1)[None],
        grad_out[None],
        gains[1][None],
        grad_gate[None],
        grad_up[None],
        grad_down[None],
    )


def solution(mesh):
    weight = P("section", "fsdp", None)
    gain = P("section", "fsdp")
    ends = P("section", None, "dp", "fsdp", None)
    return jax.shard_map(
        body,
        mesh=mesh,
        in_specs=(
            ends,
            P(None, "dp", "fsdp"),
            gain,
            weight,
            weight,
            weight,
            weight,
            gain,
            weight,
            weight,
            weight,
        ),
        out_specs=(
            ends,
            gain,
            weight,
            weight,
            weight,
            weight,
            gain,
            weight,
            weight,
            weight,
        ),
        check_vma=False,
    )
```

```python
import jax
import jax.numpy as jnp
from jax import lax
from jax.experimental import pallas as pl
from jax.experimental.pallas import tpu as pltpu
from jax.sharding import PartitionSpec as P

HEAD_DIM = 64
GROUP = 4
EPSILON = 1e-05
ROPE_THETA = 500000.0
NEGATIVE = -1e30
LANES = 128
CHUNK_ROWS = 512
CHUNK_COLS = 1024
STREAMS = 2
LEAD = 3
ATTEND_AT = 4
LOWER_AT = 15
FAR_WITH = 7
VMEM = 56 * 1024 * 1024
BF = jnp.bfloat16
F32 = jnp.float32


def mm(left, right):
    return lax.dot_general(left, right, (((1,), (0,)), ((), ())), preferred_element_type=F32)


def mm_tn(left, right):
    return lax.dot_general(left, right, (((0,), (0,)), ((), ())), preferred_element_type=F32)


def mm_nt(left, right):
    return lax.dot_general(left, right, (((1,), (1,)), ((), ())), preferred_element_type=F32)


def rms_inverse(vector):
    return lax.rsqrt(jnp.mean(vector * vector, axis=-1, keepdims=True) + EPSILON)


def turn(tile, cosine, sine, lane):
    swapped = jnp.where(
        lane % HEAD_DIM < HEAD_DIM // 2,
        pltpu.roll(tile, LANES - HEAD_DIM // 2, axis=1),
        pltpu.roll(tile, HEAD_DIM // 2, axis=1),
    )
    return tile * cosine + swapped * sine


def project_kernel(a_ref, w_ref, cos_ref, sin_ref, q_ref, pair_ref):
    step = pl.program_id(0)
    value = mm(a_ref[...], w_ref[...])
    cosine, sine = cos_ref[...], sin_ref[...]
    lane = lax.broadcasted_iota(jnp.int32, cosine.shape, 1)
    tiles = [value[:, at : at + LANES] for at in range(0, value.shape[1], LANES)]

    @pl.when(step < pl.num_programs(0) - 2)
    def _():
        for index, tile in enumerate(tiles):
            q_ref[:, index * LANES : (index + 1) * LANES] = turn(tile, cosine, sine, lane).astype(BF)

    @pl.when(step >= pl.num_programs(0) - 2)
    def _():
        for index, tile in enumerate(tiles):
            if index % 2 == 0:
                tile = turn(tile, cosine, sine, lane)
            pair_ref[:, index * LANES : (index + 1) * LANES] = tile.astype(BF)


def project(a, weights, cosine, sine, key_width):
    rows, width = a.shape
    total = weights.shape[1]
    tile = key_width
    steps = total // tile
    own = pl.BlockSpec((rows, LANES), lambda t: (0, 0))
    return pl.pallas_call(
        project_kernel,
        grid=(steps,),
        in_specs=[
            pl.BlockSpec((rows, width), lambda t: (0, 0)),
            pl.BlockSpec((width, tile), lambda t: (0, t)),
            own,
            own,
        ],
        out_specs=[
            pl.BlockSpec((rows, tile), lambda t: (0, jnp.minimum(t, steps - 3))),
            pl.BlockSpec((rows, tile), lambda t: (0, jnp.maximum(t - (steps - 2), 0))),
        ],
        out_shape=[
            jax.ShapeDtypeStruct((rows, total - 2 * key_width), BF),
            jax.ShapeDtypeStruct((rows, 2 * key_width), BF),
        ],
        compiler_params=pltpu.CompilerParams(vmem_limit_bytes=VMEM),
        cost_estimate=pl.CostEstimate(flops=1, bytes_accessed=1, transcendentals=0),
    )(a, weights, cosine, sine)


def mm(left, right):
    return lax.dot_general(left, right, (((1,), (0,)), ((), ())), preferred_element_type=F32)


def mm_nt(left, right):
    return lax.dot_general(left, right, (((1,), (1,)), ((), ())), preferred_element_type=F32)


def side_by_side(block):
    turned = block.T
    count = block.shape[1] // HEAD_DIM
    return jnp.concatenate(
        [turned[h * HEAD_DIM : (h + 1) * HEAD_DIM] for h in range(count)], axis=1
    )


def stacked(block):
    count = block.shape[1] // HEAD_DIM
    return jnp.concatenate(
        [block[:, h * HEAD_DIM : (h + 1) * HEAD_DIM] for h in range(count)], axis=0
    )


def causal_scores(keys, queries_t, rows, blocks):
    scores = mm(keys, queries_t)
    tail = scores[(blocks - 1) * rows :]
    key_at = lax.broadcasted_iota(jnp.int32, tail.shape, 0)
    query_at = lax.broadcasted_iota(jnp.int32, tail.shape, 1) % rows
    tail = jnp.where(key_at <= query_at, tail, NEGATIVE)
    if blocks == 1:
        return tail
    return jnp.concatenate([scores[: (blocks - 1) * rows], tail], axis=0)


def attend_kernel(shard_ref, q_ref, kv_ref, o_ref, lse_ref):
    rows = q_ref.shape[0]
    span = GROUP * HEAD_DIM
    pair = 2 * HEAD_DIM
    for blocks in range(1, kv_ref.shape[0] // rows + 1):

        @pl.when(shard_ref[0] == blocks - 1)
        def _():
            for half in range(2):
                at = half * HEAD_DIM
                queries = q_ref[:, half * span : (half + 1) * span]
                keys = kv_ref[: blocks * rows, at : at + HEAD_DIM]
                values = kv_ref[: blocks * rows, pair + at : pair + at + HEAD_DIM]
                queries_t = side_by_side(queries) * jnp.asarray(HEAD_DIM**-0.5, BF)
                scores = causal_scores(keys, queries_t, rows, blocks)
                top = jnp.max(scores, axis=0, keepdims=True)
                weights = jnp.exp(scores - top)
                total = jnp.sum(weights, axis=0, keepdims=True)
                out_t = mm(values.T, weights.astype(BF)) / total
                out_t = jnp.concatenate(
                    [out_t[:, h * rows : (h + 1) * rows] for h in range(GROUP)], axis=0
                )
                o_ref[:, half * span : (half + 1) * span] = out_t.T.astype(BF)
                lse_ref[0, half : half + 1, :] = top + jnp.log(total)


def attend(shard, queries, pairs):
    rows, width = queries.shape
    length, pair_width = pairs.shape
    steps = pair_width // (4 * HEAD_DIM)
    span = 2 * GROUP * HEAD_DIM
    return pl.pallas_call(
        attend_kernel,
        grid_spec=pltpu.PrefetchScalarGridSpec(
            num_scalar_prefetch=1,
            grid=(steps,),
            in_specs=[
                pl.BlockSpec((rows, span), lambda p, s: (0, p)),
                pl.BlockSpec((length, 4 * HEAD_DIM), lambda p, s: (0, p)),
            ],
            out_specs=[
                pl.BlockSpec((rows, span), lambda p, s: (0, p)),
                pl.BlockSpec((1, 2, GROUP * rows), lambda p, s: (p, 0, 0)),
            ],
        ),
        out_shape=[
            jax.ShapeDtypeStruct((rows, width), BF),
            jax.ShapeDtypeStruct((steps, 2, GROUP * rows), F32),
        ],
        compiler_params=pltpu.CompilerParams(vmem_limit_bytes=VMEM),
        cost_estimate=pl.CostEstimate(flops=1, bytes_accessed=1, transcendentals=0),
    )(shard, queries, pairs)


def attend_back_kernel(
    shard_ref, q_ref, kv_ref, lse_ref, do_ref, cos_ref, sin_ref, kcos_ref, ksin_ref, dq_ref, dkv_ref
):
    rows = q_ref.shape[0]
    span = GROUP * HEAD_DIM
    pair = 2 * HEAD_DIM
    wide = HEAD_DIM // 2
    scale = HEAD_DIM**-0.5
    for blocks in range(1, kv_ref.shape[0] // rows + 1):

        @pl.when(shard_ref[0] == blocks - 1)
        def _():
            seen = blocks * rows
            key_grads = []
            for half in range(2):
                at = half * HEAD_DIM
                queries = q_ref[:, half * span : (half + 1) * span]
                grads = do_ref[:, half * span : (half + 1) * span]
                keys = kv_ref[:seen, at : at + HEAD_DIM]
                values = kv_ref[:seen, pair + at : pair + at + HEAD_DIM]
                queries_t = side_by_side(queries) * jnp.asarray(scale, BF)
                grads_t = side_by_side(grads)
                scores = causal_scores(keys, queries_t, rows, blocks)
                weights = jnp.exp(scores - lse_ref[0, half : half + 1, :])
                moved = mm(values, grads_t)
                product = weights * moved
                delta = jnp.sum(product, axis=0, keepdims=True)
                grad_scores = (product - weights * delta).astype(BF)
                dkv_ref[:seen, pair + at : pair + at + HEAD_DIM] = mm(
                    weights.astype(BF), stacked(grads)
                ).astype(BF)
                key_grads.append(mm(grad_scores, stacked(queries)) * scale)
                grad_t = mm(keys.T, grad_scores) * scale
                turned = []
                for h in range(GROUP):
                    block = grad_t[:, h * rows : (h + 1) * rows]
                    first, second = block[:wide], block[wide:]
                    turned.append(first * cos_ref[...] + second * sin_ref[...])
                    turned.append(second * cos_ref[...] - first * sin_ref[...])
                dq_ref[:, half * span : (half + 1) * span] = (
                    jnp.concatenate(turned, axis=0).T.astype(BF)
                )
            key_grads = jnp.concatenate(key_grads, axis=1)
            lane = lax.broadcasted_iota(jnp.int32, key_grads.shape, 1)
            dkv_ref[:seen, :pair] = turn(
                key_grads, kcos_ref[:seen, :], -ksin_ref[:seen, :], lane
            ).astype(BF)
            if seen < kv_ref.shape[0]:
                dkv_ref[seen:, :] = jnp.zeros((kv_ref.shape[0] - seen, 2 * pair), BF)


def attend_back(shard, queries, pairs, lse, grads, cosine, sine, key_cosine, key_sine):
    rows, width = queries.shape
    length, pair_width = pairs.shape
    steps = pair_width // (4 * HEAD_DIM)
    span = 2 * GROUP * HEAD_DIM
    table = pl.BlockSpec((HEAD_DIM // 2, rows), lambda p, s: (0, 0))
    key_table = pl.BlockSpec((length, LANES), lambda p, s: (0, 0))
    return pl.pallas_call(
        attend_back_kernel,
        grid_spec=pltpu.PrefetchScalarGridSpec(
            num_scalar_prefetch=1,
            grid=(steps,),
            in_specs=[
                pl.BlockSpec((rows, span), lambda p, s: (0, p)),
                pl.BlockSpec((length, 4 * HEAD_DIM), lambda p, s: (0, p)),
                pl.BlockSpec((1, 2, GROUP * rows), lambda p, s: (p, 0, 0)),
                pl.BlockSpec((rows, span), lambda p, s: (0, p)),
                table,
                table,
                key_table,
                key_table,
            ],
            out_specs=[
                pl.BlockSpec((rows, span), lambda p, s: (0, p)),
                pl.BlockSpec((length, 4 * HEAD_DIM), lambda p, s: (0, p)),
            ],
        ),
        out_shape=[
            jax.ShapeDtypeStruct((rows, width), BF),
            jax.ShapeDtypeStruct((length, pair_width), BF),
        ],
        compiler_params=pltpu.CompilerParams(vmem_limit_bytes=VMEM),
        cost_estimate=pl.CostEstimate(flops=1, bytes_accessed=1, transcendentals=0),
    )(shard, queries, pairs, lse, grads, cosine, sine, key_cosine, key_sine)


def widen_kernel(shard_ref, b_ref, *refs):
    gates, ups = refs[:4], refs[4:8]
    z_ref, g_ref, u_ref = refs[8:]
    depth = gates[0].shape[0]
    gate = up = None
    for k in range(4):
        at = pl.multiple_of((shard_ref[0] ^ k) * depth, depth)
        left = b_ref[:, pl.ds(at, depth)]
        g, u = mm(left, gates[k][...]), mm(left, ups[k][...])
        gate, up = (g, u) if gate is None else (gate + g, up + u)
    z_ref[...] = (gate * jax.nn.sigmoid(gate) * up).astype(BF)
    g_ref[...] = gate.astype(BF)
    u_ref[...] = up.astype(BF)


def widen(shard, b, gates, ups, tile=512):
    rows, width = b.shape
    depth, hidden = gates[0].shape
    out = pl.BlockSpec((rows, tile), lambda t, s: (0, t))
    return pl.pallas_call(
        widen_kernel,
        grid_spec=pltpu.PrefetchScalarGridSpec(
            num_scalar_prefetch=1,
            grid=(hidden // tile,),
            in_specs=[pl.BlockSpec((rows, width), lambda t, s: (0, 0))]
            + [pl.BlockSpec((depth, tile), lambda t, s: (0, t))] * 8,
            out_specs=[out] * 3,
        ),
        out_shape=[jax.ShapeDtypeStruct((rows, hidden), BF)] * 3,
        compiler_params=pltpu.CompilerParams(vmem_limit_bytes=VMEM),
        cost_estimate=pl.CostEstimate(flops=1, bytes_accessed=1, transcendentals=0),
    )(shard, b, *gates, *ups)


def narrow_kernel(shard_ref, z_ref, m_ref, *refs):
    downs, y_ref = refs[:4], refs[4]
    depth = downs[0].shape[0]
    total = m_ref[...]
    for k in range(4):
        at = pl.multiple_of((shard_ref[0] ^ k) * depth, depth)
        total = total + mm(z_ref[:, pl.ds(at, depth)], downs[k][...])
    y_ref[...] = total


def narrow(shard, z, m, downs, tile=256):
    rows, hidden = z.shape
    depth, width = downs[0].shape
    block = pl.BlockSpec((rows, tile), lambda t, s: (0, t))
    return pl.pallas_call(
        narrow_kernel,
        grid_spec=pltpu.PrefetchScalarGridSpec(
            num_scalar_prefetch=1,
            grid=(width // tile,),
            in_specs=[pl.BlockSpec((rows, hidden), lambda t, s: (0, 0)), block]
            + [pl.BlockSpec((depth, tile), lambda t, s: (0, t))] * 4,
            out_specs=block,
        ),
        out_shape=jax.ShapeDtypeStruct((rows, width), F32),
        compiler_params=pltpu.CompilerParams(vmem_limit_bytes=VMEM),
        cost_estimate=pl.CostEstimate(flops=1, bytes_accessed=1, transcendentals=0),
    )(shard, z, m, *downs)


def hidden_back_kernel(shard_ref, dy_ref, g_ref, u_ref, *refs):
    downs, gates, ups = refs[:4], refs[4:8], refs[8:12]
    dg_ref, du_ref, db_ref, total = refs[12:]
    step = pl.program_id(0)
    per = pl.num_programs(0) // 4
    depth = gates[0].shape[0]

    def one(down):
        dz = mm_nt(dy_ref[...], down[...])
        gate = g_ref[...].astype(F32)
        up = u_ref[...].astype(F32)
        slope = jax.nn.sigmoid(gate)
        dg = (dz * up * slope * (1.0 + gate * (1.0 - slope))).astype(BF)
        du = (dz * gate * slope).astype(BF)
        dg_ref[...] = dg
        du_ref[...] = du
        for k in range(4):
            part = mm_nt(dg, gates[k][...]) + mm_nt(du, ups[k][...])
            at = pl.multiple_of((shard_ref[0] ^ k) * depth, depth)

            @pl.when(step == 0)
            def _():
                total[:, pl.ds(at, depth)] = part

            @pl.when(step > 0)
            def _():
                total[:, pl.ds(at, depth)] += part

    for k in range(4):

        @pl.when(step // per == k)
        def _():
            one(downs[k])

    @pl.when(step == pl.num_programs(0) - 1)
    def _():
        db_ref[...] = total[...]


def hidden_back(shard, dy, g, u, downs, gates, ups, tile=512):
    rows, width = dy.shape
    hidden = g.shape[1]
    depth = gates[0].shape[0]
    per = hidden // 4 // tile

    def natural(t, s):
        return (0, (s[0] ^ (t // per)) * per + t % per)

    def piece(k):
        return lambda t, s: (jnp.clip(t - k * per, 0, per - 1), 0)

    cols = pl.BlockSpec((rows, tile), natural)
    whole = pl.BlockSpec((rows, width), lambda t, s: (0, 0))
    return pl.pallas_call(
        hidden_back_kernel,
        grid_spec=pltpu.PrefetchScalarGridSpec(
            num_scalar_prefetch=1,
            grid=(hidden // tile,),
            in_specs=[whole, cols, cols]
            + [pl.BlockSpec((tile, width), piece(k)) for k in range(4)]
            + [pl.BlockSpec((depth, tile), natural)] * 8,
            out_specs=[cols, cols, whole],
            scratch_shapes=[pltpu.VMEM((rows, width), F32)],
        ),
        out_shape=[
            jax.ShapeDtypeStruct((rows, hidden), BF),
            jax.ShapeDtypeStruct((rows, hidden), BF),
            jax.ShapeDtypeStruct((rows, width), F32),
        ],
        compiler_params=pltpu.CompilerParams(vmem_limit_bytes=VMEM),
        cost_estimate=pl.CostEstimate(flops=1, bytes_accessed=1, transcendentals=0),
    )(shard, dy, g, u, *downs, *gates, *ups)


def outer(x, row, parts, column, width, added=None, earlier=(), span=0, tile=512):
    per = (span or width) // tile
    count = width // tile // per
    first = column // tile
    at = row // CHUNK_ROWS
    held = [] if added is None else [added]
    extra = list(earlier)

    def kernel(*refs):
        step = pl.program_id(0)
        left = jnp.concatenate([part[...] for part in refs[: len(x)]], axis=1)
        refs = refs[len(x) :]
        right = jnp.concatenate([part[...] for part in refs[: len(parts)]], axis=0)
        value = mm(left, right)
        if held:
            value = value + refs[len(parts)][...].astype(F32)
        for index in range(count):

            @pl.when(step // per == index)
            def _():
                refs[len(parts) + len(held) + len(extra) + index][...] = value.astype(BF)

    def chunk(index):
        return lambda t: (0, jnp.clip(t - index * per, 0, per - 1))

    return pl.pallas_call(
        kernel,
        grid=(count * per,),
        in_specs=[pl.BlockSpec((CHUNK_ROWS, part.shape[1]), lambda t: (at, 0)) for part in x]
        + [pl.BlockSpec((part.shape[0], tile), lambda t: (0, first + t)) for part in parts]
        + [pl.BlockSpec((CHUNK_ROWS, tile), lambda t: (0, t))] * len(held)
        + [pl.BlockSpec(memory_space=pl.ANY)] * len(extra),
        out_specs=[pl.BlockSpec((CHUNK_ROWS, tile), chunk(index)) for index in range(count)],
        out_shape=[jax.ShapeDtypeStruct((CHUNK_ROWS, per * tile), BF)] * count,
        compiler_params=pltpu.CompilerParams(vmem_limit_bytes=VMEM),
        cost_estimate=pl.CostEstimate(flops=1, bytes_accessed=1, transcendentals=0),
    )(*x, *parts, *held, *extra)


def core_swap(x):
    return lax.ppermute(x, "fsdp", [(0, 1), (1, 0), (2, 3), (3, 2)])


def chip_swap(x):
    return lax.ppermute(x, "fsdp", [(0, 2), (2, 0), (1, 3), (3, 1)])


def after(value, other):
    always = lax.axis_index("dp") > -7
    return jnp.where(always, value, other.reshape(-1)[0].astype(value.dtype))


def nothing_kernel(*refs):
    pass


def hold(x, *others):
    anywhere = pl.BlockSpec(memory_space=pl.ANY)
    return pl.pallas_call(
        nothing_kernel,
        in_specs=[anywhere] * (1 + len(others)),
        out_specs=anywhere,
        out_shape=jax.ShapeDtypeStruct(x.shape, x.dtype),
        input_output_aliases={0: 0},
        compiler_params=pltpu.CompilerParams(vmem_limit_bytes=VMEM),
        cost_estimate=pl.CostEstimate(flops=1, bytes_accessed=1, transcendentals=0),
    )(x, *others)


def turned_kernel(shard_ref, *refs):
    for k in range(4):
        refs[4 + k][...] = refs[k][...].T


def turned_blocks(shard, x, tile=512):
    rows, width = x.shape
    per = width // 4 // tile

    def block(k):
        return pl.BlockSpec((rows, tile), lambda t, s: (0, (s[0] ^ k) * per + t))

    return pl.pallas_call(
        turned_kernel,
        grid_spec=pltpu.PrefetchScalarGridSpec(
            num_scalar_prefetch=1,
            grid=(per,),
            in_specs=[block(k) for k in range(4)],
            out_specs=[pl.BlockSpec((tile, rows), lambda t, s: (t, 0))] * 4,
        ),
        out_shape=[jax.ShapeDtypeStruct((width // 4, rows), x.dtype)] * 4,
        compiler_params=pltpu.CompilerParams(vmem_limit_bytes=VMEM),
        cost_estimate=pl.CostEstimate(flops=1, bytes_accessed=1, transcendentals=0),
    )(shard, x, x, x, x)


def column_block(x, index, width):
    return lax.dynamic_slice_in_dim(x, index * width, width, axis=1)


def relay_kernel(names, places, root, place_ref, *refs):
    named = dict(zip(names, refs))
    up_ref, down_ref = refs[-2:]
    place = place_ref[0]

    def read(name):
        return named[name][...].astype(F32) if name in named else 0.0

    own = 0.0
    for name, held_by in places:
        if name not in named:
            continue
        mine = held_by[0] == place
        for position in held_by[1:]:
            mine = mine | (place == position)
        own = jnp.where(mine, named[name][...].astype(F32), own)
    total = own + read("below_held") + read("above_held")
    up = jnp.where(place == root, total, read("below") + jnp.where(place < root, own, 0.0))
    down = jnp.where(place == root, total, read("above") + jnp.where(place > root, own, 0.0))
    up_ref[...] = jnp.broadcast_to(up, up_ref.shape).astype(up_ref.dtype)
    down_ref[...] = jnp.broadcast_to(down, down_ref.shape).astype(down_ref.dtype)


def relay(place, root, places, operands, earlier, shape, kind):
    names = [name for name in operands if operands[name] is not None]
    unique, at = [], {}
    for name in names:
        for index, other in enumerate(unique):
            if operands[name] is other:
                at[name] = index
        if name not in at:
            at[name] = len(unique)
            unique.append(operands[name])
    rows, cols = shape
    tile = rows // 2 if rows >= 256 else rows
    block = pl.BlockSpec((tile, cols), lambda t, s: (t, 0))

    def kernel(place_ref, *refs):
        values = refs[: len(unique)]
        relay_kernel(names, places, root, place_ref, *[values[at[n]] for n in names], *refs[-2:])

    return pl.pallas_call(
        kernel,
        grid_spec=pltpu.PrefetchScalarGridSpec(
            num_scalar_prefetch=1,
            grid=(rows // tile,),
            in_specs=[block] * len(unique) + [pl.BlockSpec(memory_space=pl.ANY)] * len(earlier),
            out_specs=[block, block],
        ),
        out_shape=[jax.ShapeDtypeStruct(shape, kind)] * 2,
        compiler_params=pltpu.CompilerParams(vmem_limit_bytes=VMEM),
        cost_estimate=pl.CostEstimate(flops=1, bytes_accessed=1, transcendentals=0),
    )(place, *unique, *earlier)


def replica_chain(count, make, shape, kind, stream_count=STREAMS, wanted=None):
    peers = lax.axis_size("dp")
    place = lax.axis_index("dp")
    place_vector = place.astype(jnp.int32).reshape(1)
    root = (peers - 1) // 2
    delay = max(root, peers - 1 - root)
    counts = [len(range(q, count, stream_count)) for q in range(stream_count)]
    streams = [[] for _ in counts]
    ups = [[] for _ in streams]
    downs = [[] for _ in streams]
    sent = [[] for _ in streams]
    order = []
    lags = [
        position if position < root else delay if position == root else peers - 1 - position
        for position in range(peers)
    ]

    def nth(items, index):
        return items[index] if 0 <= index < len(items) else None

    def going(position, direction, step):
        if (root - position) * direction > 0:
            return step - lags[position]
        return step - delay - abs(position - root)

    for step in range(max(counts) + 2 * delay):
        for q in range(stream_count):
            if step >= counts[q] + 2 * delay:
                continue
            if wanted is not None and order:
                wanted(len(order), order[-1][0])
            if step < counts[q]:
                before = (order[-LEAD][0],) if len(order) >= LEAD else ()
                streams[q].append(make(q + step * stream_count, before))
            places, operands = [], {}
            for lag in sorted(set(lags)):
                name = f"own{lag}"
                operands[name] = nth(streams[q], step - lag)
                places.append((name, [p for p in range(peers) if lags[p] == lag]))
            operands["below"] = nth(ups[q], step - 1)
            operands["above"] = nth(downs[q], step - 1)
            operands["below_held"] = nth(ups[q], step - 1 - (delay - root))
            operands["above_held"] = nth(downs[q], step - 1 - (delay - (peers - 1 - root)))
            earlier = ()
            if stream_count > 1 and len(order) > stream_count:
                earlier = order[-(stream_count + 1)]
            up, down = relay(place_vector, root, places, operands, earlier, shape, kind)
            sent[q].append((up, down))
            if step < counts[q] + 2 * delay - 1:
                up_pairs = [(i, i + 1) for i in range(peers - 1) if 0 <= going(i, 1, step) < counts[q]]
                down_pairs = [(i, i - 1) for i in range(1, peers) if 0 <= going(i, -1, step) < counts[q]]
                ups[q].append(lax.ppermute(up, "dp", up_pairs))
                downs[q].append(lax.ppermute(down, "dp", down_pairs))
                order.append((ups[q][-1], downs[q][-1]))
    distance = jnp.abs(place - root)
    totals = [None] * count
    for q in range(stream_count):
        for index in range(counts[q]):
            total = None
            for hops in range(delay + 1):
                up, down = sent[q][index + delay + hops]
                value = jnp.where(place >= root, up, down)
                total = value if total is None else jnp.where(distance == hops, value, total)
            totals[q + index * stream_count] = total
    return totals


def body(
    ends, positions, attn_gain, w_query, w_key, w_value, w_out, mlp_gain, w_gate, w_up, w_down
):
    shard = lax.axis_index("fsdp")
    shard_vector = shard.astype(jnp.int32).reshape(1)
    replica = lax.axis_index("dp")
    replicas = lax.axis_size("dp")
    first_section = lax.axis_index("section") == 0
    tok_rows = ends.shape[3]
    model_width = ends.shape[4]
    length = tok_rows * lax.axis_size("fsdp")
    key_width = w_key.shape[2]
    query_width = w_query.shape[2]
    ends_local = ends[0, :, 0]

    gains = lax.all_gather(
        jnp.concatenate([attn_gain, mlp_gain], axis=0), "fsdp", axis=1, tiled=True
    ).astype(F32)
    gain_attn, gain_mlp = gains[0], gains[1]
    places_all = lax.all_gather(positions[:, 0], "fsdp", axis=1, tiled=True)
    start = gain_attn[0] + places_all[0, 0].astype(F32)

    def rotary(micro_first, micro_second):
        places = jnp.where(first_section, places_all[micro_first], places_all[micro_second])
        half = HEAD_DIM // 2
        frequency = jnp.exp(-jnp.log(ROPE_THETA) * 2.0 * jnp.arange(half, dtype=F32) / HEAD_DIM)
        angles = places.astype(F32)[:, None] * frequency[None, :]
        cosine, sine = jnp.cos(angles), jnp.sin(angles)
        own = [lax.dynamic_slice_in_dim(x, shard * tok_rows, tok_rows, 0) for x in (cosine, sine)]
        lanes = LANES // HEAD_DIM
        wide = (
            jnp.tile(cosine, (1, 2 * lanes)),
            jnp.tile(jnp.concatenate([-sine, sine], axis=1), (1, lanes)),
        )
        wide_own = [lax.dynamic_slice_in_dim(x, shard * tok_rows, tok_rows, 0) for x in wide]
        return wide_own, (own[0].T, own[1].T), wide

    table_a = rotary(1, 0)
    table_b = rotary(0, 1)

    def part(x):
        rows = x.shape[0] // replicas
        return lax.dynamic_slice_in_dim(x, replica * rows, rows, axis=0)

    def spread(x):
        return lax.all_gather(x, "dp", axis=0, tiled=True)

    pieces = [w_query[0]]
    for at in range(0, key_width, LANES):
        pieces += [w_key[0, :, at : at + LANES], w_value[0, :, at : at + LANES]]
    own_qkv = jnp.concatenate(pieces, axis=1)
    own_out, own_gate, own_up, own_down = w_out[0], w_gate[0], w_up[0], w_down[0]
    middle = own_gate.shape[1] // 2
    sends = [part(own_gate[:, :middle]), own_qkv, part(own_gate[:, middle:])]
    sends += [part(own_out), part(own_up)]
    got = []
    spreads = []
    for index, send in enumerate(sends):
        send = after(send, got[-1] if got else start)
        if index == 4:
            send = after(send, spreads[0])
        got.append(chip_swap(send))
        if index != 1:
            spreads.append(spread(got[-1]))

    def shards(own, other):
        return (own, core_swap(own), other, core_swap(other))

    def natural(values):
        rows = values[0].shape[0]
        whole = jnp.zeros((4 * rows, values[0].shape[1]), BF)
        for k, value in enumerate(values):
            whole = lax.dynamic_update_slice(whole, value, ((shard ^ k) * rows, 0))
        return whole

    gates = shards(own_gate, jnp.concatenate(spreads[:2], axis=1))
    mat_qkv = natural(shards(own_qkv, got[1]))
    mat_out = natural(shards(own_out, spreads[2]))

    def all_rows(x):
        return shards(x, chip_swap(x))

    def summed_rows(x):
        def rows_of(index):
            return lax.dynamic_slice_in_dim(x, index * tok_rows, tok_rows, 0)

        near = rows_of(shard).astype(F32) + core_swap(rows_of(shard ^ 1)).astype(F32)
        far = rows_of(shard ^ 2).astype(F32) + core_swap(rows_of(shard ^ 3)).astype(F32)
        return (near + chip_swap(far.astype(BF)).astype(F32)).astype(BF)

    def enter(layer_input, table):
        inverse_one = rms_inverse(layer_input)
        normed_attn = (layer_input * inverse_one * gain_attn).astype(BF)
        queries, pairs = project(normed_attn, mat_qkv, *table[0], key_width)
        return inverse_one, normed_attn, queries, natural(all_rows(pairs))

    def middle_part(layer_input, entered, *waits):
        held = shard_vector
        for other in waits:
            held = after(held, other)
        attended, log_totals = attend(held, entered[2], entered[3])
        residual_mid = layer_input + mm(attended, mat_out)
        inverse_two = rms_inverse(residual_mid)
        normed_mlp = (residual_mid * inverse_two * gain_mlp).astype(BF)
        return attended, log_totals, residual_mid, inverse_two, normed_mlp

    def leave(layer_input, entered, halfway, widened=None):
        inverse_one, normed_attn, queries, pairs_all = entered
        attended, log_totals, residual_mid, inverse_two, normed_mlp = halfway
        widened = widened or widen(shard_vector, normed_mlp, gates, ups)
        hidden_act, gate_pre, up_proj = widened
        output = narrow(shard_vector, hidden_act, residual_mid, downs)
        return output, {
            "input": layer_input,
            "inverse_one": inverse_one,
            "a": normed_attn,
            "queries": queries,
            "pairs": pairs_all,
            "log": log_totals,
            "o": attended,
            "mid": residual_mid,
            "inverse_two": inverse_two,
            "b": normed_mlp,
            "gate": gate_pre,
            "up": up_proj,
            "z": hidden_act,
        }

    def back_upper(grad_top, saved):
        grad_gate_pre, grad_up_proj, grad_normed = hidden_back(
            shard_vector, grad_top, saved["gate"], saved["up"], downs, gates, ups
        )
        inverse_two = saved["inverse_two"]
        base_mid = saved["mid"] * inverse_two
        part_gain_mlp = jnp.sum(grad_normed * base_mid, axis=0)
        scaled_grad = grad_normed * gain_mlp
        grad_mid = grad_top.astype(F32) + inverse_two * (
            scaled_grad - base_mid * jnp.mean(scaled_grad * base_mid, axis=-1, keepdims=True)
        )
        attn_grad = grad_mid.astype(BF)
        return grad_gate_pre, grad_up_proj, attn_grad, grad_mid, part_gain_mlp

    def back_attention(upper, saved, table, *waits):
        held = shard_vector
        for other in waits:
            held = after(held, other)
        grad_attended = mm_nt(upper[2], mat_out).astype(BF)
        grad_queries, grad_pairs = attend_back(
            held, saved["queries"], saved["pairs"], saved["log"], grad_attended, *table[1], *table[2]
        )

        def rows_of(index):
            return lax.dynamic_slice_in_dim(grad_pairs, index * tok_rows, tok_rows, 0)

        far = rows_of(shard ^ 2).astype(F32) + core_swap(rows_of(shard ^ 3)).astype(F32)
        far = far.astype(BF)
        near = rows_of(shard).astype(F32) + core_swap(rows_of(shard ^ 1)).astype(F32)
        return grad_queries, near, far

    def back_lower(upper, attention, saved, far=None):
        grad_queries, near, sent = attention
        far = chip_swap(sent) if far is None else far
        grad_qkv = jnp.concatenate([grad_queries, (near + far.astype(F32)).astype(BF)], axis=1)
        grad_normed = mm_nt(grad_qkv, mat_qkv)
        base_in = saved["input"] * saved["inverse_one"]
        part_gain_attn = jnp.sum(grad_normed * base_in, axis=0)
        scaled_grad = grad_normed * gain_attn
        grad_in = upper[3] + saved["inverse_one"] * (
            scaled_grad - base_in * jnp.mean(scaled_grad * base_in, axis=-1, keepdims=True)
        )
        return grad_in, grad_qkv, jnp.stack([part_gain_attn, upper[4]])

    def ahead(x):
        return lax.ppermute(x.astype(BF), "section", [(0, 1)])

    def back(x):
        return lax.ppermute(x.astype(BF), "section", [(1, 0)])

    def choose(first, second):
        return jnp.where(first_section, first, second)

    layer_input = ends_local[0].astype(F32)
    entered = enter(layer_input, table_b)
    other_down = chip_swap(after(after(own_down, got[-1]), entered[3]))
    halfway = middle_part(layer_input, entered)
    ups = shards(own_up, hold(spreads[3], halfway[4]))
    downs = shards(own_down, hold(other_down, halfway[4]))
    output, _ = leave(layer_input, entered, halfway)
    received = ahead(output)
    layer_input = choose(ends_local[1], received).astype(F32)
    entered = enter(layer_input, table_a)
    output_one, saved_a = leave(layer_input, entered, middle_part(layer_input, entered))
    received = ahead(output_one)
    turned_a = turned_blocks(shard_vector, saved_a["z"])
    layer_input = choose(ends_local[0], received).astype(F32)
    entered = enter(layer_input, table_b)
    halfway = middle_part(layer_input, entered, turned_a[0])
    output_two, saved_b = leave(layer_input, entered, halfway)
    turned_b = turned_blocks(shard_vector, saved_b["z"])

    def shares(blocks_a, blocks_b):
        near = (blocks_a[0], blocks_b[0], core_swap(blocks_a[1]), core_swap(blocks_b[1]))
        far = (blocks_a[2], blocks_b[2], core_swap(blocks_a[3]), core_swap(blocks_b[3]))
        return near, far

    def shares_of(name):
        return shares(
            turned_blocks(shard_vector, saved_a[name]), turned_blocks(shard_vector, saved_b[name])
        )

    def chip_rows(first, second):
        return (first, second, core_swap(first), core_swap(second))

    upper = back_upper(ends_local[0], saved_a)
    grad_in, _, _ = back_lower(upper, back_attention(upper, saved_a, table_a), saved_a)
    received = back(grad_in)
    top_b = choose(received, ends_local[1])
    upper_b = back_upper(top_b, saved_b)
    attention = back_attention(upper_b, saved_b, table_b)
    grad_one, grad_qkv_b, gains_b = back_lower(upper_b, attention, saved_b)
    received = back(grad_one)
    shared = {name: shares_of(name) for name in ("b", "o", "a")}
    received = hold(received, output_two, *[shared[name][1][0] for name in ("b", "o", "a")])
    top_a = choose(received, ends_local[0])

    late = {"down": (shares(turned_a, turned_b), chip_rows(top_a, top_b))}
    work = {}
    crossed = []

    def begin_last(begun):
        work["upper"] = upper_a = back_upper(after(top_a, begun), saved_a)
        late["gate"] = (shared["b"], chip_rows(upper_a[0], upper_b[0]))
        late["up"] = (shared["b"], chip_rows(upper_a[1], upper_b[1]))
        late["out"] = (shared["o"], chip_rows(upper_a[2], upper_b[2]))

    def wanted(sends, last):
        if sends == ATTEND_AT:
            work["attention"] = back_attention(work["upper"], saved_a, table_a, last)
        if sends == LOWER_AT:
            far = crossed[FAR_WITH][CHUNK_ROWS:, : work["attention"][2].shape[1]]
            work["done"] = back_lower(work["upper"], work["attention"], saved_a, far)
            late["attn"] = (shared["a"], chip_rows(work["done"][1], grad_qkv_b))
            gains = work["done"][2] + gains_b
            gains = (gains + core_swap(gains)).astype(BF)
            block = model_width // 4
            own, other = column_block(gains, shard, block), column_block(gains, shard ^ 2, block)
            gains = own.astype(F32) + chip_swap(other).astype(F32)
            spare = ((0, CHUNK_ROWS - gains.shape[0]), (0, CHUNK_COLS - block))
            work["gains"] = jnp.pad(gains, spare).astype(BF)

    pair = 2 * CHUNK_COLS
    hidden_width = w_gate.shape[2]
    qkv_width = query_width + 2 * key_width
    plan = []
    for row in range(0, w_down.shape[1], CHUNK_ROWS):
        plan += [("down", row, col, pair) for col in range(0, model_width, pair)]
    for name, width in (("gate", hidden_width), ("up", hidden_width), ("out", model_width)):
        plan += [(name, 0, col, pair) for col in range(0, width, pair)]
    plan += [("attn", 0, col, min(pair, qkv_width - col)) for col in range(0, qkv_width, pair)]
    made = []

    def cross(earlier):
        name, row, col, width = plan[len(crossed)]
        (own, other), parts = late[name]
        (result,) = outer(other, row, parts, col, width, None, earlier)
        if len(crossed) == FAR_WITH:
            far = work["attention"][2]
            far = jnp.pad(far, ((0, 0), (0, result.shape[1] - far.shape[1])))
            result = jnp.concatenate([result, far], axis=0)
        crossed.append(chip_swap(result))
        return result

    def make(index, earlier):
        if index == count - 1:
            return work["gains"]
        if index == len(made):
            at = index // 2
            if index == 0:
                cross(())
                begin_last(cross(()))
                earlier = (work["upper"][0],)
            name, row, col, width = plan[at]
            (own, other), parts = late[name]
            made.extend(outer(own, row, parts, col, width, crossed[at], earlier, CHUNK_COLS))
        elif len(crossed) < len(plan):
            cross(earlier)
        return made[index]

    count = sum(width // CHUNK_COLS for _, _, _, width in plan) + 1
    totals = replica_chain(count, make, (CHUNK_ROWS, CHUNK_COLS), BF, wanted=wanted)
    grad_two = work["done"][0]

    gains = totals.pop()[: gains_b.shape[0], : model_width // 4].astype(F32)

    def assembled(rows, cols):
        count = (rows // CHUNK_ROWS) * (cols // CHUNK_COLS)
        taken, totals[:] = totals[:count], totals[count:]
        across = cols // CHUNK_COLS
        lines = [
            jnp.concatenate(taken[at : at + across], axis=1) for at in range(0, count, across)
        ]
        return jnp.concatenate(lines, axis=0).astype(F32)

    grad_down = assembled(w_down.shape[1], w_down.shape[2])
    grad_gate = assembled(w_gate.shape[1], w_gate.shape[2])
    grad_up = assembled(w_up.shape[1], w_up.shape[2])
    grad_out = assembled(w_out.shape[1], w_out.shape[2])
    grad_qkv = assembled(w_query.shape[1], qkv_width)
    grad_pairs = [
        grad_qkv[:, at : at + LANES] for at in range(query_width, grad_qkv.shape[1], LANES)
    ]
    boundary = choose(jnp.stack([grad_one, grad_two]), jnp.stack([output_one, output_two]))
    return (
        boundary[None, :, None],
        gains[0][None],
        grad_qkv[:, :query_width][None],
        jnp.concatenate(grad_pairs[::2], axis=1)[None],
        jnp.concatenate(grad_pairs[1::2], axis=1)[None],
        grad_out[None],
        gains[1][None],
        grad_gate[None],
        grad_up[None],
        grad_down[None],
    )


def solution(mesh):
    weight = P("section", "fsdp", None)
    gain = P("section", "fsdp")
    ends = P("section", None, "dp", "fsdp", None)
    return jax.shard_map(
        body,
        mesh=mesh,
        in_specs=(
            ends,
            P(None, "dp", "fsdp"),
            gain,
            weight,
            weight,
            weight,
            weight,
            gain,
            weight,
            weight,
            weight,
        ),
        out_specs=(
            ends,
            gain,
            weight,
            weight,
            weight,
            weight,
            gain,
            weight,
            weight,
            weight,
        ),
        check_vma=False,
    )
```

```python
import jax
import jax.numpy as jnp
from jax import lax
from jax.experimental import pallas as pl
from jax.experimental.pallas import tpu as pltpu
from jax.sharding import PartitionSpec as P

HEAD_DIM = 64
GROUP = 4
EPSILON = 1e-05
ROPE_THETA = 500000.0
NEGATIVE = -1e30
LANES = 128
CHUNK_ROWS = 512
CHUNK_COLS = 1024
STREAMS = 2
LEAD = 3
ATTEND_AT = 4
LOWER_AT = 15
FAR_WITH = 7
VMEM = 56 * 1024 * 1024
BF = jnp.bfloat16
F32 = jnp.float32


def mm(left, right):
    return lax.dot_general(left, right, (((1,), (0,)), ((), ())), preferred_element_type=F32)


def mm_tn(left, right):
    return lax.dot_general(left, right, (((0,), (0,)), ((), ())), preferred_element_type=F32)


def mm_nt(left, right):
    return lax.dot_general(left, right, (((1,), (1,)), ((), ())), preferred_element_type=F32)


def rms_inverse(vector):
    return lax.rsqrt(jnp.mean(vector * vector, axis=-1, keepdims=True) + EPSILON)


def turn(tile, cosine, sine, lane):
    swapped = jnp.where(
        lane % HEAD_DIM < HEAD_DIM // 2,
        pltpu.roll(tile, LANES - HEAD_DIM // 2, axis=1),
        pltpu.roll(tile, HEAD_DIM // 2, axis=1),
    )
    return tile * cosine + swapped * sine


def project_kernel(a_ref, w_ref, cos_ref, sin_ref, q_ref, pair_ref):
    step = pl.program_id(0)
    value = mm(a_ref[...], w_ref[...])
    cosine, sine = cos_ref[...], sin_ref[...]
    lane = lax.broadcasted_iota(jnp.int32, cosine.shape, 1)
    tiles = [value[:, at : at + LANES] for at in range(0, value.shape[1], LANES)]

    @pl.when(step < pl.num_programs(0) - 2)
    def _():
        for index, tile in enumerate(tiles):
            q_ref[:, index * LANES : (index + 1) * LANES] = turn(tile, cosine, sine, lane).astype(BF)

    @pl.when(step >= pl.num_programs(0) - 2)
    def _():
        for index, tile in enumerate(tiles):
            if index % 2 == 0:
                tile = turn(tile, cosine, sine, lane)
            pair_ref[:, index * LANES : (index + 1) * LANES] = tile.astype(BF)


def project(a, weights, cosine, sine, key_width):
    rows, width = a.shape
    total = weights.shape[1]
    tile = key_width
    steps = total // tile
    own = pl.BlockSpec((rows, LANES), lambda t: (0, 0))
    return pl.pallas_call(
        project_kernel,
        grid=(steps,),
        in_specs=[
            pl.BlockSpec((rows, width), lambda t: (0, 0)),
            pl.BlockSpec((width, tile), lambda t: (0, t)),
            own,
            own,
        ],
        out_specs=[
            pl.BlockSpec((rows, tile), lambda t: (0, jnp.minimum(t, steps - 3))),
            pl.BlockSpec((rows, tile), lambda t: (0, jnp.maximum(t - (steps - 2), 0))),
        ],
        out_shape=[
            jax.ShapeDtypeStruct((rows, total - 2 * key_width), BF),
            jax.ShapeDtypeStruct((rows, 2 * key_width), BF),
        ],
        compiler_params=pltpu.CompilerParams(vmem_limit_bytes=VMEM),
        cost_estimate=pl.CostEstimate(flops=1, bytes_accessed=1, transcendentals=0),
    )(a, weights, cosine, sine)


def mm(left, right):
    return lax.dot_general(left, right, (((1,), (0,)), ((), ())), preferred_element_type=F32)


def mm_nt(left, right):
    return lax.dot_general(left, right, (((1,), (1,)), ((), ())), preferred_element_type=F32)


def side_by_side(block):
    turned = block.T
    count = block.shape[1] // HEAD_DIM
    return jnp.concatenate(
        [turned[h * HEAD_DIM : (h + 1) * HEAD_DIM] for h in range(count)], axis=1
    )


def stacked(block):
    count = block.shape[1] // HEAD_DIM
    return jnp.concatenate(
        [block[:, h * HEAD_DIM : (h + 1) * HEAD_DIM] for h in range(count)], axis=0
    )


def causal_scores(keys, queries_t, rows, blocks):
    scores = mm(keys, queries_t)
    tail = scores[(blocks - 1) * rows :]
    key_at = lax.broadcasted_iota(jnp.int32, tail.shape, 0)
    query_at = lax.broadcasted_iota(jnp.int32, tail.shape, 1) % rows
    tail = jnp.where(key_at <= query_at, tail, NEGATIVE)
    if blocks == 1:
        return tail
    return jnp.concatenate([scores[: (blocks - 1) * rows], tail], axis=0)


def attend_kernel(shard_ref, q_ref, kv_ref, o_ref, lse_ref):
    rows = q_ref.shape[0]
    span = GROUP * HEAD_DIM
    pair = 2 * HEAD_DIM
    for blocks in range(1, kv_ref.shape[0] // rows + 1):

        @pl.when(shard_ref[0] == blocks - 1)
        def _():
            for half in range(2):
                at = half * HEAD_DIM
                queries = q_ref[:, half * span : (half + 1) * span]
                keys = kv_ref[: blocks * rows, at : at + HEAD_DIM]
                values = kv_ref[: blocks * rows, pair + at : pair + at + HEAD_DIM]
                queries_t = side_by_side(queries) * jnp.asarray(HEAD_DIM**-0.5, BF)
                scores = causal_scores(keys, queries_t, rows, blocks)
                top = jnp.max(scores, axis=0, keepdims=True)
                weights = jnp.exp(scores - top)
                total = jnp.sum(weights, axis=0, keepdims=True)
                out_t = mm(values.T, weights.astype(BF)) / total
                out_t = jnp.concatenate(
                    [out_t[:, h * rows : (h + 1) * rows] for h in range(GROUP)], axis=0
                )
                o_ref[:, half * span : (half + 1) * span] = out_t.T.astype(BF)
                lse_ref[0, half : half + 1, :] = top + jnp.log(total)


def attend(shard, queries, pairs):
    rows, width = queries.shape
    length, pair_width = pairs.shape
    steps = pair_width // (4 * HEAD_DIM)
    span = 2 * GROUP * HEAD_DIM
    return pl.pallas_call(
        attend_kernel,
        grid_spec=pltpu.PrefetchScalarGridSpec(
            num_scalar_prefetch=1,
            grid=(steps,),
            in_specs=[
                pl.BlockSpec((rows, span), lambda p, s: (0, p)),
                pl.BlockSpec((length, 4 * HEAD_DIM), lambda p, s: (0, p)),
            ],
            out_specs=[
                pl.BlockSpec((rows, span), lambda p, s: (0, p)),
                pl.BlockSpec((1, 2, GROUP * rows), lambda p, s: (p, 0, 0)),
            ],
        ),
        out_shape=[
            jax.ShapeDtypeStruct((rows, width), BF),
            jax.ShapeDtypeStruct((steps, 2, GROUP * rows), F32),
        ],
        compiler_params=pltpu.CompilerParams(vmem_limit_bytes=VMEM),
        cost_estimate=pl.CostEstimate(flops=1, bytes_accessed=1, transcendentals=0),
    )(shard, queries, pairs)


def attend_back_kernel(
    shard_ref, q_ref, kv_ref, lse_ref, do_ref, cos_ref, sin_ref, kcos_ref, ksin_ref, dq_ref, dkv_ref
):
    rows = q_ref.shape[0]
    span = GROUP * HEAD_DIM
    pair = 2 * HEAD_DIM
    wide = HEAD_DIM // 2
    scale = HEAD_DIM**-0.5
    for blocks in range(1, kv_ref.shape[0] // rows + 1):

        @pl.when(shard_ref[0] == blocks - 1)
        def _():
            seen = blocks * rows
            key_grads = []
            for half in range(2):
                at = half * HEAD_DIM
                queries = q_ref[:, half * span : (half + 1) * span]
                grads = do_ref[:, half * span : (half + 1) * span]
                keys = kv_ref[:seen, at : at + HEAD_DIM]
                values = kv_ref[:seen, pair + at : pair + at + HEAD_DIM]
                queries_t = side_by_side(queries) * jnp.asarray(scale, BF)
                grads_t = side_by_side(grads)
                scores = causal_scores(keys, queries_t, rows, blocks)
                weights = jnp.exp(scores - lse_ref[0, half : half + 1, :])
                moved = mm(values, grads_t)
                product = weights * moved
                delta = jnp.sum(product, axis=0, keepdims=True)
                grad_scores = (product - weights * delta).astype(BF)
                dkv_ref[:seen, pair + at : pair + at + HEAD_DIM] = mm(
                    weights.astype(BF), stacked(grads)
                ).astype(BF)
                key_grads.append(mm(grad_scores, stacked(queries)) * scale)
                grad_t = mm(keys.T, grad_scores) * scale
                turned = []
                for h in range(GROUP):
                    block = grad_t[:, h * rows : (h + 1) * rows]
                    first, second = block[:wide], block[wide:]
                    turned.append(first * cos_ref[...] + second * sin_ref[...])
                    turned.append(second * cos_ref[...] - first * sin_ref[...])
                dq_ref[:, half * span : (half + 1) * span] = (
                    jnp.concatenate(turned, axis=0).T.astype(BF)
                )
            key_grads = jnp.concatenate(key_grads, axis=1)
            lane = lax.broadcasted_iota(jnp.int32, key_grads.shape, 1)
            dkv_ref[:seen, :pair] = turn(
                key_grads, kcos_ref[:seen, :], -ksin_ref[:seen, :], lane
            ).astype(BF)
            if seen < kv_ref.shape[0]:
                dkv_ref[seen:, :] = jnp.zeros((kv_ref.shape[0] - seen, 2 * pair), BF)


def attend_back(shard, queries, pairs, lse, grads, cosine, sine, key_cosine, key_sine):
    rows, width = queries.shape
    length, pair_width = pairs.shape
    steps = pair_width // (4 * HEAD_DIM)
    span = 2 * GROUP * HEAD_DIM
    table = pl.BlockSpec((HEAD_DIM // 2, rows), lambda p, s: (0, 0))
    key_table = pl.BlockSpec((length, LANES), lambda p, s: (0, 0))
    return pl.pallas_call(
        attend_back_kernel,
        grid_spec=pltpu.PrefetchScalarGridSpec(
            num_scalar_prefetch=1,
            grid=(steps,),
            in_specs=[
                pl.BlockSpec((rows, span), lambda p, s: (0, p)),
                pl.BlockSpec((length, 4 * HEAD_DIM), lambda p, s: (0, p)),
                pl.BlockSpec((1, 2, GROUP * rows), lambda p, s: (p, 0, 0)),
                pl.BlockSpec((rows, span), lambda p, s: (0, p)),
                table,
                table,
                key_table,
                key_table,
            ],
            out_specs=[
                pl.BlockSpec((rows, span), lambda p, s: (0, p)),
                pl.BlockSpec((length, 4 * HEAD_DIM), lambda p, s: (0, p)),
            ],
        ),
        out_shape=[
            jax.ShapeDtypeStruct((rows, width), BF),
            jax.ShapeDtypeStruct((length, pair_width), BF),
        ],
        compiler_params=pltpu.CompilerParams(vmem_limit_bytes=VMEM),
        cost_estimate=pl.CostEstimate(flops=1, bytes_accessed=1, transcendentals=0),
    )(shard, queries, pairs, lse, grads, cosine, sine, key_cosine, key_sine)


def widen_kernel(shard_ref, b_ref, *refs):
    gates, ups = refs[:4], refs[4:8]
    z_ref, g_ref, u_ref = refs[8:]
    depth = gates[0].shape[0]
    gate = up = None
    for k in range(4):
        at = pl.multiple_of((shard_ref[0] ^ k) * depth, depth)
        left = b_ref[:, pl.ds(at, depth)]
        g, u = mm(left, gates[k][...]), mm(left, ups[k][...])
        gate, up = (g, u) if gate is None else (gate + g, up + u)
    z_ref[...] = (gate * jax.nn.sigmoid(gate) * up).astype(BF)
    g_ref[...] = gate.astype(BF)
    u_ref[...] = up.astype(BF)


def widen(shard, b, gates, ups, tile=512):
    rows, width = b.shape
    depth, hidden = gates[0].shape
    out = pl.BlockSpec((rows, tile), lambda t, s: (0, t))
    return pl.pallas_call(
        widen_kernel,
        grid_spec=pltpu.PrefetchScalarGridSpec(
            num_scalar_prefetch=1,
            grid=(hidden // tile,),
            in_specs=[pl.BlockSpec((rows, width), lambda t, s: (0, 0))]
            + [pl.BlockSpec((depth, tile), lambda t, s: (0, t))] * 8,
            out_specs=[out] * 3,
        ),
        out_shape=[jax.ShapeDtypeStruct((rows, hidden), BF)] * 3,
        compiler_params=pltpu.CompilerParams(vmem_limit_bytes=VMEM),
        cost_estimate=pl.CostEstimate(flops=1, bytes_accessed=1, transcendentals=0),
    )(shard, b, *gates, *ups)


def narrow_kernel(shard_ref, z_ref, m_ref, *refs):
    downs, y_ref = refs[:4], refs[4]
    depth = downs[0].shape[0]
    total = m_ref[...]
    for k in range(4):
        at = pl.multiple_of((shard_ref[0] ^ k) * depth, depth)
        total = total + mm(z_ref[:, pl.ds(at, depth)], downs[k][...])
    y_ref[...] = total


def narrow(shard, z, m, downs, tile=256):
    rows, hidden = z.shape
    depth, width = downs[0].shape
    block = pl.BlockSpec((rows, tile), lambda t, s: (0, t))
    return pl.pallas_call(
        narrow_kernel,
        grid_spec=pltpu.PrefetchScalarGridSpec(
            num_scalar_prefetch=1,
            grid=(width // tile,),
            in_specs=[pl.BlockSpec((rows, hidden), lambda t, s: (0, 0)), block]
            + [pl.BlockSpec((depth, tile), lambda t, s: (0, t))] * 4,
            out_specs=block,
        ),
        out_shape=jax.ShapeDtypeStruct((rows, width), F32),
        compiler_params=pltpu.CompilerParams(vmem_limit_bytes=VMEM),
        cost_estimate=pl.CostEstimate(flops=1, bytes_accessed=1, transcendentals=0),
    )(shard, z, m, *downs)


def hidden_back_kernel(shard_ref, dy_ref, g_ref, u_ref, *refs):
    downs, gates, ups = refs[:4], refs[4:8], refs[8:12]
    dg_ref, du_ref, db_ref, total = refs[12:]
    step = pl.program_id(0)
    per = pl.num_programs(0) // 4
    depth = gates[0].shape[0]

    def one(down):
        dz = mm_nt(dy_ref[...], down[...])
        gate = g_ref[...].astype(F32)
        up = u_ref[...].astype(F32)
        slope = jax.nn.sigmoid(gate)
        dg = (dz * up * slope * (1.0 + gate * (1.0 - slope))).astype(BF)
        du = (dz * gate * slope).astype(BF)
        dg_ref[...] = dg
        du_ref[...] = du
        for k in range(4):
            part = mm_nt(dg, gates[k][...]) + mm_nt(du, ups[k][...])
            at = pl.multiple_of((shard_ref[0] ^ k) * depth, depth)

            @pl.when(step == 0)
            def _():
                total[:, pl.ds(at, depth)] = part

            @pl.when(step > 0)
            def _():
                total[:, pl.ds(at, depth)] += part

    for k in range(4):

        @pl.when(step // per == k)
        def _():
            one(downs[k])

    @pl.when(step == pl.num_programs(0) - 1)
    def _():
        db_ref[...] = total[...]


def hidden_back(shard, dy, g, u, downs, gates, ups, tile=512):
    rows, width = dy.shape
    hidden = g.shape[1]
    depth = gates[0].shape[0]
    per = hidden // 4 // tile

    def natural(t, s):
        return (0, (s[0] ^ (t // per)) * per + t % per)

    def piece(k):
        return lambda t, s: (jnp.clip(t - k * per, 0, per - 1), 0)

    cols = pl.BlockSpec((rows, tile), natural)
    whole = pl.BlockSpec((rows, width), lambda t, s: (0, 0))
    return pl.pallas_call(
        hidden_back_kernel,
        grid_spec=pltpu.PrefetchScalarGridSpec(
            num_scalar_prefetch=1,
            grid=(hidden // tile,),
            in_specs=[whole, cols, cols]
            + [pl.BlockSpec((tile, width), piece(k)) for k in range(4)]
            + [pl.BlockSpec((depth, tile), natural)] * 8,
            out_specs=[cols, cols, whole],
            scratch_shapes=[pltpu.VMEM((rows, width), F32)],
        ),
        out_shape=[
            jax.ShapeDtypeStruct((rows, hidden), BF),
            jax.ShapeDtypeStruct((rows, hidden), BF),
            jax.ShapeDtypeStruct((rows, width), F32),
        ],
        compiler_params=pltpu.CompilerParams(vmem_limit_bytes=VMEM),
        cost_estimate=pl.CostEstimate(flops=1, bytes_accessed=1, transcendentals=0),
    )(shard, dy, g, u, *downs, *gates, *ups)


def outer(x, row, parts, column, width, added=None, earlier=(), span=0, tile=512):
    per = (span or width) // tile
    count = width // tile // per
    first = column // tile
    at = row // CHUNK_ROWS
    held = [] if added is None else [added]
    extra = list(earlier)

    def kernel(*refs):
        step = pl.program_id(0)
        left = jnp.concatenate([part[...] for part in refs[: len(x)]], axis=1)
        refs = refs[len(x) :]
        right = jnp.concatenate([part[...] for part in refs[: len(parts)]], axis=0)
        value = mm(left, right)
        if held:
            value = value + refs[len(parts)][...].astype(F32)
        for index in range(count):

            @pl.when(step // per == index)
            def _():
                refs[len(parts) + len(held) + len(extra) + index][...] = value.astype(BF)

    def chunk(index):
        return lambda t: (0, jnp.clip(t - index * per, 0, per - 1))

    return pl.pallas_call(
        kernel,
        grid=(count * per,),
        in_specs=[pl.BlockSpec((CHUNK_ROWS, part.shape[1]), lambda t: (at, 0)) for part in x]
        + [pl.BlockSpec((part.shape[0], tile), lambda t: (0, first + t)) for part in parts]
        + [pl.BlockSpec((CHUNK_ROWS, tile), lambda t: (0, t))] * len(held)
        + [pl.BlockSpec(memory_space=pl.ANY)] * len(extra),
        out_specs=[pl.BlockSpec((CHUNK_ROWS, tile), chunk(index)) for index in range(count)],
        out_shape=[jax.ShapeDtypeStruct((CHUNK_ROWS, per * tile), BF)] * count,
        compiler_params=pltpu.CompilerParams(vmem_limit_bytes=VMEM),
        cost_estimate=pl.CostEstimate(flops=1, bytes_accessed=1, transcendentals=0),
    )(*x, *parts, *held, *extra)


def core_swap(x):
    return lax.ppermute(x, "fsdp", [(0, 1), (1, 0), (2, 3), (3, 2)])


def chip_swap(x):
    return lax.ppermute(x, "fsdp", [(0, 2), (2, 0), (1, 3), (3, 1)])


def after(value, other):
    always = lax.axis_index("dp") > -7
    return jnp.where(always, value, other.reshape(-1)[0].astype(value.dtype))


def nothing_kernel(*refs):
    pass


def hold(x, *others):
    anywhere = pl.BlockSpec(memory_space=pl.ANY)
    return pl.pallas_call(
        nothing_kernel,
        in_specs=[anywhere] * (1 + len(others)),
        out_specs=anywhere,
        out_shape=jax.ShapeDtypeStruct(x.shape, x.dtype),
        input_output_aliases={0: 0},
        compiler_params=pltpu.CompilerParams(vmem_limit_bytes=VMEM),
        cost_estimate=pl.CostEstimate(flops=1, bytes_accessed=1, transcendentals=0),
    )(x, *others)


def turned_kernel(shard_ref, *refs):
    for k in range(4):
        refs[4 + k][...] = refs[k][...].T


def turned_blocks(shard, x, tile=512):
    rows, width = x.shape
    per = width // 4 // tile

    def block(k):
        return pl.BlockSpec((rows, tile), lambda t, s: (0, (s[0] ^ k) * per + t))

    return pl.pallas_call(
        turned_kernel,
        grid_spec=pltpu.PrefetchScalarGridSpec(
            num_scalar_prefetch=1,
            grid=(per,),
            in_specs=[block(k) for k in range(4)],
            out_specs=[pl.BlockSpec((tile, rows), lambda t, s: (t, 0))] * 4,
        ),
        out_shape=[jax.ShapeDtypeStruct((width // 4, rows), x.dtype)] * 4,
        compiler_params=pltpu.CompilerParams(vmem_limit_bytes=VMEM),
        cost_estimate=pl.CostEstimate(flops=1, bytes_accessed=1, transcendentals=0),
    )(shard, x, x, x, x)


def column_block(x, index, width):
    return lax.dynamic_slice_in_dim(x, index * width, width, axis=1)


def relay_kernel(names, places, root, place_ref, *refs):
    named = dict(zip(names, refs))
    up_ref, down_ref = refs[-2:]
    place = place_ref[0]

    def read(name):
        return named[name][...].astype(F32) if name in named else 0.0

    own = 0.0
    for name, held_by in places:
        if name not in named:
            continue
        mine = held_by[0] == place
        for position in held_by[1:]:
            mine = mine | (place == position)
        own = jnp.where(mine, named[name][...].astype(F32), own)
    total = own + read("below_held") + read("above_held")
    up = jnp.where(place == root, total, read("below") + jnp.where(place < root, own, 0.0))
    down = jnp.where(place == root, total, read("above") + jnp.where(place > root, own, 0.0))
    up_ref[...] = jnp.broadcast_to(up, up_ref.shape).astype(up_ref.dtype)
    down_ref[...] = jnp.broadcast_to(down, down_ref.shape).astype(down_ref.dtype)


def relay(place, root, places, operands, earlier, shape, kind):
    names = [name for name in operands if operands[name] is not None]
    unique, at = [], {}
    for name in names:
        for index, other in enumerate(unique):
            if operands[name] is other:
                at[name] = index
        if name not in at:
            at[name] = len(unique)
            unique.append(operands[name])
    rows, cols = shape
    tile = rows // 2 if rows >= 256 else rows
    block = pl.BlockSpec((tile, cols), lambda t, s: (t, 0))

    def kernel(place_ref, *refs):
        values = refs[: len(unique)]
        relay_kernel(names, places, root, place_ref, *[values[at[n]] for n in names], *refs[-2:])

    return pl.pallas_call(
        kernel,
        grid_spec=pltpu.PrefetchScalarGridSpec(
            num_scalar_prefetch=1,
            grid=(rows // tile,),
            in_specs=[block] * len(unique) + [pl.BlockSpec(memory_space=pl.ANY)] * len(earlier),
            out_specs=[block, block],
        ),
        out_shape=[jax.ShapeDtypeStruct(shape, kind)] * 2,
        compiler_params=pltpu.CompilerParams(vmem_limit_bytes=VMEM),
        cost_estimate=pl.CostEstimate(flops=1, bytes_accessed=1, transcendentals=0),
    )(place, *unique, *earlier)


def replica_chain(count, make, shape, kind, stream_count=STREAMS, wanted=None):
    peers = lax.axis_size("dp")
    place = lax.axis_index("dp")
    place_vector = place.astype(jnp.int32).reshape(1)
    root = (peers - 1) // 2
    delay = max(root, peers - 1 - root)
    counts = [len(range(q, count, stream_count)) for q in range(stream_count)]
    streams = [[] for _ in counts]
    ups = [[] for _ in streams]
    downs = [[] for _ in streams]
    sent = [[] for _ in streams]
    order = []
    lags = [
        position if position < root else delay if position == root else peers - 1 - position
        for position in range(peers)
    ]

    def nth(items, index):
        return items[index] if 0 <= index < len(items) else None

    def going(position, direction, step):
        if (root - position) * direction > 0:
            return step - lags[position]
        return step - delay - abs(position - root)

    for step in range(max(counts) + 2 * delay):
        for q in range(stream_count):
            if step >= counts[q] + 2 * delay:
                continue
            if wanted is not None and order:
                wanted(len(order), order[-1][0])
            if step < counts[q]:
                before = (order[-LEAD][0],) if len(order) >= LEAD else ()
                streams[q].append(make(q + step * stream_count, before))
            places, operands = [], {}
            for lag in sorted(set(lags)):
                name = f"own{lag}"
                operands[name] = nth(streams[q], step - lag)
                places.append((name, [p for p in range(peers) if lags[p] == lag]))
            operands["below"] = nth(ups[q], step - 1)
            operands["above"] = nth(downs[q], step - 1)
            operands["below_held"] = nth(ups[q], step - 1 - (delay - root))
            operands["above_held"] = nth(downs[q], step - 1 - (delay - (peers - 1 - root)))
            earlier = ()
            if stream_count > 1 and len(order) > stream_count:
                earlier = order[-(stream_count + 1)]
            up, down = relay(place_vector, root, places, operands, earlier, shape, kind)
            sent[q].append((up, down))
            if step < counts[q] + 2 * delay - 1:
                up_pairs = [(i, i + 1) for i in range(peers - 1) if 0 <= going(i, 1, step) < counts[q]]
                down_pairs = [(i, i - 1) for i in range(1, peers) if 0 <= going(i, -1, step) < counts[q]]
                ups[q].append(lax.ppermute(up, "dp", up_pairs))
                downs[q].append(lax.ppermute(down, "dp", down_pairs))
                order.append((ups[q][-1], downs[q][-1]))
    choice = 2 * jnp.abs(place - root) + (place < root).astype(jnp.int32)
    found = []
    for index in range(count):
        at, q = divmod(index, stream_count)
        found.append([x for hops in range(delay + 1) for x in sent[q][at + delay + hops]])
    return choice.astype(jnp.int32).reshape(1), found


def place_chunk(choice, found, whole, shape, row, column, tile=128):
    per = CHUNK_ROWS // tile
    kept = [] if whole is None else [whole]

    def kernel(choice_ref, *refs):
        for index in range(len(found)):

            @pl.when(choice_ref[0] == index)
            def _():
                refs[-1][...] = refs[index][...].astype(F32)

    def chosen(index):
        return lambda t, s: (jnp.where(s[0] == index, t, 0), 0)

    return pl.pallas_call(
        kernel,
        grid_spec=pltpu.PrefetchScalarGridSpec(
            num_scalar_prefetch=1,
            grid=(per,),
            in_specs=[pl.BlockSpec((tile, CHUNK_COLS), chosen(k)) for k in range(len(found))]
            + [pl.BlockSpec(memory_space=pl.ANY)] * len(kept),
            out_specs=pl.BlockSpec((tile, CHUNK_COLS), lambda t, s: (row * per + t, column)),
        ),
        out_shape=jax.ShapeDtypeStruct(shape, F32),
        input_output_aliases={1 + len(found): 0} if kept else {},
        compiler_params=pltpu.CompilerParams(vmem_limit_bytes=VMEM),
        cost_estimate=pl.CostEstimate(flops=1, bytes_accessed=1, transcendentals=0),
    )(choice, *found, *kept)


def body(
    ends, positions, attn_gain, w_query, w_key, w_value, w_out, mlp_gain, w_gate, w_up, w_down
):
    shard = lax.axis_index("fsdp")
    shard_vector = shard.astype(jnp.int32).reshape(1)
    replica = lax.axis_index("dp")
    replicas = lax.axis_size("dp")
    first_section = lax.axis_index("section") == 0
    tok_rows = ends.shape[3]
    model_width = ends.shape[4]
    length = tok_rows * lax.axis_size("fsdp")
    key_width = w_key.shape[2]
    query_width = w_query.shape[2]
    ends_local = ends[0, :, 0]

    gains = lax.all_gather(
        jnp.concatenate([attn_gain, mlp_gain], axis=0), "fsdp", axis=1, tiled=True
    ).astype(F32)
    gain_attn, gain_mlp = gains[0], gains[1]
    places_all = lax.all_gather(positions[:, 0], "fsdp", axis=1, tiled=True)
    start = gain_attn[0] + places_all[0, 0].astype(F32)

    def rotary(micro_first, micro_second):
        places = jnp.where(first_section, places_all[micro_first], places_all[micro_second])
        half = HEAD_DIM // 2
        frequency = jnp.exp(-jnp.log(ROPE_THETA) * 2.0 * jnp.arange(half, dtype=F32) / HEAD_DIM)
        angles = places.astype(F32)[:, None] * frequency[None, :]
        cosine, sine = jnp.cos(angles), jnp.sin(angles)
        own = [lax.dynamic_slice_in_dim(x, shard * tok_rows, tok_rows, 0) for x in (cosine, sine)]
        lanes = LANES // HEAD_DIM
        wide = (
            jnp.tile(cosine, (1, 2 * lanes)),
            jnp.tile(jnp.concatenate([-sine, sine], axis=1), (1, lanes)),
        )
        wide_own = [lax.dynamic_slice_in_dim(x, shard * tok_rows, tok_rows, 0) for x in wide]
        return wide_own, (own[0].T, own[1].T), wide

    table_a = rotary(1, 0)
    table_b = rotary(0, 1)

    def part(x):
        rows = x.shape[0] // replicas
        return lax.dynamic_slice_in_dim(x, replica * rows, rows, axis=0)

    def spread(x):
        return lax.all_gather(x, "dp", axis=0, tiled=True)

    pieces = [w_query[0]]
    for at in range(0, key_width, LANES):
        pieces += [w_key[0, :, at : at + LANES], w_value[0, :, at : at + LANES]]
    own_qkv = jnp.concatenate(pieces, axis=1)
    own_out, own_gate, own_up, own_down = w_out[0], w_gate[0], w_up[0], w_down[0]
    middle = own_gate.shape[1] // 2
    sends = [part(own_gate[:, :middle]), own_qkv, part(own_gate[:, middle:])]
    sends += [part(own_out), part(own_up)]
    got = []
    spreads = []
    for index, send in enumerate(sends):
        send = after(send, got[-1] if got else start)
        if index == 4:
            send = after(send, spreads[0])
        got.append(chip_swap(send))
        if index != 1:
            spreads.append(spread(got[-1]))

    def shards(own, other):
        return (own, core_swap(own), other, core_swap(other))

    def natural(values):
        rows = values[0].shape[0]
        whole = jnp.zeros((4 * rows, values[0].shape[1]), BF)
        for k, value in enumerate(values):
            whole = lax.dynamic_update_slice(whole, value, ((shard ^ k) * rows, 0))
        return whole

    gates = shards(own_gate, jnp.concatenate(spreads[:2], axis=1))
    mat_qkv = natural(shards(own_qkv, got[1]))
    mat_out = natural(shards(own_out, spreads[2]))

    def all_rows(x):
        return shards(x, chip_swap(x))

    def summed_rows(x):
        def rows_of(index):
            return lax.dynamic_slice_in_dim(x, index * tok_rows, tok_rows, 0)

        near = rows_of(shard).astype(F32) + core_swap(rows_of(shard ^ 1)).astype(F32)
        far = rows_of(shard ^ 2).astype(F32) + core_swap(rows_of(shard ^ 3)).astype(F32)
        return (near + chip_swap(far.astype(BF)).astype(F32)).astype(BF)

    def enter(layer_input, table):
        inverse_one = rms_inverse(layer_input)
        normed_attn = (layer_input * inverse_one * gain_attn).astype(BF)
        queries, pairs = project(normed_attn, mat_qkv, *table[0], key_width)
        return inverse_one, normed_attn, queries, natural(all_rows(pairs))

    def middle_part(layer_input, entered, *waits):
        held = shard_vector
        for other in waits:
            held = after(held, other)
        attended, log_totals = attend(held, entered[2], entered[3])
        residual_mid = layer_input + mm(attended, mat_out)
        inverse_two = rms_inverse(residual_mid)
        normed_mlp = (residual_mid * inverse_two * gain_mlp).astype(BF)
        return attended, log_totals, residual_mid, inverse_two, normed_mlp

    def leave(layer_input, entered, halfway, widened=None):
        inverse_one, normed_attn, queries, pairs_all = entered
        attended, log_totals, residual_mid, inverse_two, normed_mlp = halfway
        widened = widened or widen(shard_vector, normed_mlp, gates, ups)
        hidden_act, gate_pre, up_proj = widened
        output = narrow(shard_vector, hidden_act, residual_mid, downs)
        return output, {
            "input": layer_input,
            "inverse_one": inverse_one,
            "a": normed_attn,
            "queries": queries,
            "pairs": pairs_all,
            "log": log_totals,
            "o": attended,
            "mid": residual_mid,
            "inverse_two": inverse_two,
            "b": normed_mlp,
            "gate": gate_pre,
            "up": up_proj,
            "z": hidden_act,
        }

    def back_upper(grad_top, saved):
        grad_gate_pre, grad_up_proj, grad_normed = hidden_back(
            shard_vector, grad_top, saved["gate"], saved["up"], downs, gates, ups
        )
        inverse_two = saved["inverse_two"]
        base_mid = saved["mid"] * inverse_two
        part_gain_mlp = jnp.sum(grad_normed * base_mid, axis=0)
        scaled_grad = grad_normed * gain_mlp
        grad_mid = grad_top.astype(F32) + inverse_two * (
            scaled_grad - base_mid * jnp.mean(scaled_grad * base_mid, axis=-1, keepdims=True)
        )
        attn_grad = grad_mid.astype(BF)
        return grad_gate_pre, grad_up_proj, attn_grad, grad_mid, part_gain_mlp

    def back_attention(upper, saved, table, *waits):
        held = shard_vector
        for other in waits:
            held = after(held, other)
        grad_attended = mm_nt(upper[2], mat_out).astype(BF)
        grad_queries, grad_pairs = attend_back(
            held, saved["queries"], saved["pairs"], saved["log"], grad_attended, *table[1], *table[2]
        )

        def rows_of(index):
            return lax.dynamic_slice_in_dim(grad_pairs, index * tok_rows, tok_rows, 0)

        far = rows_of(shard ^ 2).astype(F32) + core_swap(rows_of(shard ^ 3)).astype(F32)
        far = far.astype(BF)
        near = rows_of(shard).astype(F32) + core_swap(rows_of(shard ^ 1)).astype(F32)
        return grad_queries, near, far

    def back_lower(upper, attention, saved, far=None):
        grad_queries, near, sent = attention
        far = chip_swap(sent) if far is None else far
        grad_qkv = jnp.concatenate([grad_queries, (near + far.astype(F32)).astype(BF)], axis=1)
        grad_normed = mm_nt(grad_qkv, mat_qkv)
        base_in = saved["input"] * saved["inverse_one"]
        part_gain_attn = jnp.sum(grad_normed * base_in, axis=0)
        scaled_grad = grad_normed * gain_attn
        grad_in = upper[3] + saved["inverse_one"] * (
            scaled_grad - base_in * jnp.mean(scaled_grad * base_in, axis=-1, keepdims=True)
        )
        return grad_in, grad_qkv, jnp.stack([part_gain_attn, upper[4]])

    def ahead(x):
        return lax.ppermute(x.astype(BF), "section", [(0, 1)])

    def back(x):
        return lax.ppermute(x.astype(BF), "section", [(1, 0)])

    def choose(first, second):
        return jnp.where(first_section, first, second)

    layer_input = ends_local[0].astype(F32)
    entered = enter(layer_input, table_b)
    other_down = chip_swap(after(after(own_down, got[-1]), entered[3]))
    halfway = middle_part(layer_input, entered)
    ups = shards(own_up, hold(spreads[3], halfway[4]))
    downs = shards(own_down, hold(other_down, halfway[4]))
    output, _ = leave(layer_input, entered, halfway)
    received = ahead(output)
    layer_input = choose(ends_local[1], received).astype(F32)
    entered = enter(layer_input, table_a)
    output_one, saved_a = leave(layer_input, entered, middle_part(layer_input, entered))
    received = ahead(output_one)
    turned_a = turned_blocks(shard_vector, saved_a["z"])
    layer_input = choose(ends_local[0], received).astype(F32)
    entered = enter(layer_input, table_b)
    halfway = middle_part(layer_input, entered, turned_a[0])
    output_two, saved_b = leave(layer_input, entered, halfway)
    turned_b = turned_blocks(shard_vector, saved_b["z"])

    def shares(blocks_a, blocks_b):
        near = (blocks_a[0], blocks_b[0], core_swap(blocks_a[1]), core_swap(blocks_b[1]))
        far = (blocks_a[2], blocks_b[2], core_swap(blocks_a[3]), core_swap(blocks_b[3]))
        return near, far

    def shares_of(name):
        return shares(
            turned_blocks(shard_vector, saved_a[name]), turned_blocks(shard_vector, saved_b[name])
        )

    def chip_rows(first, second):
        return (first, second, core_swap(first), core_swap(second))

    upper = back_upper(ends_local[0], saved_a)
    grad_in, _, _ = back_lower(upper, back_attention(upper, saved_a, table_a), saved_a)
    received = back(grad_in)
    top_b = choose(received, ends_local[1])
    upper_b = back_upper(top_b, saved_b)
    attention = back_attention(upper_b, saved_b, table_b)
    grad_one, grad_qkv_b, gains_b = back_lower(upper_b, attention, saved_b)
    received = back(grad_one)
    shared = {name: shares_of(name) for name in ("b", "o", "a")}
    received = hold(received, output_two, *[shared[name][1][0] for name in ("b", "o", "a")])
    top_a = choose(received, ends_local[0])

    late = {"down": (shares(turned_a, turned_b), chip_rows(top_a, top_b))}
    work = {}
    crossed = []

    def begin_last(begun):
        work["upper"] = upper_a = back_upper(after(top_a, begun), saved_a)
        late["gate"] = (shared["b"], chip_rows(upper_a[0], upper_b[0]))
        late["up"] = (shared["b"], chip_rows(upper_a[1], upper_b[1]))
        late["out"] = (shared["o"], chip_rows(upper_a[2], upper_b[2]))

    def wanted(sends, last):
        if sends == ATTEND_AT:
            work["attention"] = back_attention(work["upper"], saved_a, table_a, last)
        if sends == LOWER_AT:
            far = crossed[FAR_WITH][CHUNK_ROWS:, : work["attention"][2].shape[1]]
            work["done"] = back_lower(work["upper"], work["attention"], saved_a, far)
            late["attn"] = (shared["a"], chip_rows(work["done"][1], grad_qkv_b))
            gains = work["done"][2] + gains_b
            gains = (gains + core_swap(gains)).astype(BF)
            block = model_width // 4
            own, other = column_block(gains, shard, block), column_block(gains, shard ^ 2, block)
            gains = own.astype(F32) + chip_swap(other).astype(F32)
            spare = ((0, CHUNK_ROWS - gains.shape[0]), (0, CHUNK_COLS - block))
            work["gains"] = jnp.pad(gains, spare).astype(BF)

    pair = 2 * CHUNK_COLS
    hidden_width = w_gate.shape[2]
    qkv_width = query_width + 2 * key_width
    plan = []
    for row in range(0, w_down.shape[1], CHUNK_ROWS):
        plan += [("down", row, col, pair) for col in range(0, model_width, pair)]
    for name, width in (("gate", hidden_width), ("up", hidden_width), ("out", model_width)):
        plan += [(name, 0, col, pair) for col in range(0, width, pair)]
    plan += [("attn", 0, col, min(pair, qkv_width - col)) for col in range(0, qkv_width, pair)]
    made = []

    def cross(earlier):
        name, row, col, width = plan[len(crossed)]
        (own, other), parts = late[name]
        (result,) = outer(other, row, parts, col, width, None, earlier)
        if len(crossed) == FAR_WITH:
            far = work["attention"][2]
            far = jnp.pad(far, ((0, 0), (0, result.shape[1] - far.shape[1])))
            result = jnp.concatenate([result, far], axis=0)
        crossed.append(chip_swap(result))
        return result

    def make(index, earlier):
        if index == count - 1:
            return work["gains"]
        if index == len(made):
            at = index // 2
            if index == 0:
                cross(())
                begin_last(cross(()))
                earlier = (work["upper"][0],)
            name, row, col, width = plan[at]
            (own, other), parts = late[name]
            made.extend(outer(own, row, parts, col, width, crossed[at], earlier, CHUNK_COLS))
        elif len(crossed) < len(plan):
            cross(earlier)
        return made[index]

    count = sum(width // CHUNK_COLS for _, _, _, width in plan) + 1
    choice, found = replica_chain(count, make, (CHUNK_ROWS, CHUNK_COLS), BF, wanted=wanted)
    grad_two = work["done"][0]

    last = [x[: gains_b.shape[0], : model_width // 4] for x in found.pop()]
    gains = last[0]
    for index, x in enumerate(last):
        gains = jnp.where(choice[0] == index, x, gains)
    gains = gains.astype(F32)

    def assembled(rows, cols):
        whole = None
        across = cols // CHUNK_COLS
        for index in range(rows // CHUNK_ROWS * across):
            row, column = divmod(index, across)
            whole = place_chunk(choice, found.pop(0), whole, (rows, cols), row, column)
        return whole

    grad_down = assembled(w_down.shape[1], w_down.shape[2])
    grad_gate = assembled(w_gate.shape[1], w_gate.shape[2])
    grad_up = assembled(w_up.shape[1], w_up.shape[2])
    grad_out = assembled(w_out.shape[1], w_out.shape[2])
    grad_query = assembled(w_query.shape[1], query_width)
    grad_both = assembled(w_query.shape[1], 2 * key_width)
    grad_pairs = [grad_both[:, at : at + LANES] for at in range(0, 2 * key_width, LANES)]
    boundary = choose(jnp.stack([grad_one, grad_two]), jnp.stack([output_one, output_two]))
    return (
        boundary[None, :, None],
        gains[0][None],
        grad_query[None],
        jnp.concatenate(grad_pairs[::2], axis=1)[None],
        jnp.concatenate(grad_pairs[1::2], axis=1)[None],
        grad_out[None],
        gains[1][None],
        grad_gate[None],
        grad_up[None],
        grad_down[None],
    )


def solution(mesh):
    weight = P("section", "fsdp", None)
    gain = P("section", "fsdp")
    ends = P("section", None, "dp", "fsdp", None)
    return jax.shard_map(
        body,
        mesh=mesh,
        in_specs=(
            ends,
            P(None, "dp", "fsdp"),
            gain,
            weight,
            weight,
            weight,
            weight,
            gain,
            weight,
            weight,
            weight,
        ),
        out_specs=(
            ends,
            gain,
            weight,
            weight,
            weight,
            weight,
            gain,
            weight,
            weight,
            weight,
        ),
        check_vma=False,
    )
```

```python
import jax
import jax.numpy as jnp
from jax import lax
from jax.experimental import pallas as pl
from jax.experimental.pallas import tpu as pltpu
from jax.sharding import PartitionSpec as P

HEAD_DIM = 64
GROUP = 4
EPSILON = 1e-05
ROPE_THETA = 500000.0
NEGATIVE = -1e30
LANES = 128
CHUNK_ROWS = 512
CHUNK_COLS = 1024
STREAMS = 2
LEAD = 3
ATTEND_AT = 4
LOWER_AT = 15
FAR_WITH = 7
VMEM = 56 * 1024 * 1024
BF = jnp.bfloat16
F32 = jnp.float32


def mm(left, right):
    return lax.dot_general(left, right, (((1,), (0,)), ((), ())), preferred_element_type=F32)


def mm_tn(left, right):
    return lax.dot_general(left, right, (((0,), (0,)), ((), ())), preferred_element_type=F32)


def mm_nt(left, right):
    return lax.dot_general(left, right, (((1,), (1,)), ((), ())), preferred_element_type=F32)


def rms_inverse(vector):
    return lax.rsqrt(jnp.mean(vector * vector, axis=-1, keepdims=True) + EPSILON)


def turn(tile, cosine, sine, lane):
    swapped = jnp.where(
        lane % HEAD_DIM < HEAD_DIM // 2,
        pltpu.roll(tile, LANES - HEAD_DIM // 2, axis=1),
        pltpu.roll(tile, HEAD_DIM // 2, axis=1),
    )
    return tile * cosine + swapped * sine


def project_kernel(a_ref, w_ref, cos_ref, sin_ref, q_ref, pair_ref):
    step = pl.program_id(0)
    value = mm(a_ref[...], w_ref[...])
    cosine, sine = cos_ref[...], sin_ref[...]
    lane = lax.broadcasted_iota(jnp.int32, cosine.shape, 1)
    tiles = [value[:, at : at + LANES] for at in range(0, value.shape[1], LANES)]

    @pl.when(step < pl.num_programs(0) - 2)
    def _():
        for index, tile in enumerate(tiles):
            q_ref[:, index * LANES : (index + 1) * LANES] = turn(tile, cosine, sine, lane).astype(BF)

    @pl.when(step >= pl.num_programs(0) - 2)
    def _():
        for index, tile in enumerate(tiles):
            if index % 2 == 0:
                tile = turn(tile, cosine, sine, lane)
            pair_ref[:, index * LANES : (index + 1) * LANES] = tile.astype(BF)


def project(a, weights, cosine, sine, key_width):
    rows, width = a.shape
    total = weights.shape[1]
    tile = key_width
    steps = total // tile
    own = pl.BlockSpec((rows, LANES), lambda t: (0, 0))
    return pl.pallas_call(
        project_kernel,
        grid=(steps,),
        in_specs=[
            pl.BlockSpec((rows, width), lambda t: (0, 0)),
            pl.BlockSpec((width, tile), lambda t: (0, t)),
            own,
            own,
        ],
        out_specs=[
            pl.BlockSpec((rows, tile), lambda t: (0, jnp.minimum(t, steps - 3))),
            pl.BlockSpec((rows, tile), lambda t: (0, jnp.maximum(t - (steps - 2), 0))),
        ],
        out_shape=[
            jax.ShapeDtypeStruct((rows, total - 2 * key_width), BF),
            jax.ShapeDtypeStruct((rows, 2 * key_width), BF),
        ],
        compiler_params=pltpu.CompilerParams(vmem_limit_bytes=VMEM),
        cost_estimate=pl.CostEstimate(flops=1, bytes_accessed=1, transcendentals=0),
    )(a, weights, cosine, sine)


def mm(left, right):
    return lax.dot_general(left, right, (((1,), (0,)), ((), ())), preferred_element_type=F32)


def mm_nt(left, right):
    return lax.dot_general(left, right, (((1,), (1,)), ((), ())), preferred_element_type=F32)


def side_by_side(block):
    turned = block.T
    count = block.shape[1] // HEAD_DIM
    return jnp.concatenate(
        [turned[h * HEAD_DIM : (h + 1) * HEAD_DIM] for h in range(count)], axis=1
    )


def stacked(block):
    count = block.shape[1] // HEAD_DIM
    return jnp.concatenate(
        [block[:, h * HEAD_DIM : (h + 1) * HEAD_DIM] for h in range(count)], axis=0
    )


def causal_scores(keys, queries_t, rows, blocks):
    scores = mm(keys, queries_t)
    tail = scores[(blocks - 1) * rows :]
    key_at = lax.broadcasted_iota(jnp.int32, tail.shape, 0)
    query_at = lax.broadcasted_iota(jnp.int32, tail.shape, 1) % rows
    tail = jnp.where(key_at <= query_at, tail, NEGATIVE)
    if blocks == 1:
        return tail
    return jnp.concatenate([scores[: (blocks - 1) * rows], tail], axis=0)


def attend_kernel(shard_ref, q_ref, kv_ref, o_ref, lse_ref):
    rows = q_ref.shape[0]
    span = GROUP * HEAD_DIM
    pair = 2 * HEAD_DIM
    for blocks in range(1, kv_ref.shape[0] // rows + 1):

        @pl.when(shard_ref[0] == blocks - 1)
        def _():
            for half in range(2):
                at = half * HEAD_DIM
                queries = q_ref[:, half * span : (half + 1) * span]
                keys = kv_ref[: blocks * rows, at : at + HEAD_DIM]
                values = kv_ref[: blocks * rows, pair + at : pair + at + HEAD_DIM]
                queries_t = side_by_side(queries) * jnp.asarray(HEAD_DIM**-0.5, BF)
                scores = causal_scores(keys, queries_t, rows, blocks)
                top = jnp.max(scores, axis=0, keepdims=True)
                weights = jnp.exp(scores - top)
                total = jnp.sum(weights, axis=0, keepdims=True)
                out_t = mm(values.T, weights.astype(BF)) / total
                out_t = jnp.concatenate(
                    [out_t[:, h * rows : (h + 1) * rows] for h in range(GROUP)], axis=0
                )
                o_ref[:, half * span : (half + 1) * span] = out_t.T.astype(BF)
                lse_ref[0, half : half + 1, :] = top + jnp.log(total)


def attend(shard, queries, pairs):
    rows, width = queries.shape
    length, pair_width = pairs.shape
    steps = pair_width // (4 * HEAD_DIM)
    span = 2 * GROUP * HEAD_DIM
    return pl.pallas_call(
        attend_kernel,
        grid_spec=pltpu.PrefetchScalarGridSpec(
            num_scalar_prefetch=1,
            grid=(steps,),
            in_specs=[
                pl.BlockSpec((rows, span), lambda p, s: (0, p)),
                pl.BlockSpec((length, 4 * HEAD_DIM), lambda p, s: (0, p)),
            ],
            out_specs=[
                pl.BlockSpec((rows, span), lambda p, s: (0, p)),
                pl.BlockSpec((1, 2, GROUP * rows), lambda p, s: (p, 0, 0)),
            ],
        ),
        out_shape=[
            jax.ShapeDtypeStruct((rows, width), BF),
            jax.ShapeDtypeStruct((steps, 2, GROUP * rows), F32),
        ],
        compiler_params=pltpu.CompilerParams(vmem_limit_bytes=VMEM),
        cost_estimate=pl.CostEstimate(flops=1, bytes_accessed=1, transcendentals=0),
    )(shard, queries, pairs)


def attend_back_kernel(
    shard_ref, q_ref, kv_ref, lse_ref, do_ref, cos_ref, sin_ref, kcos_ref, ksin_ref, dq_ref, dkv_ref
):
    rows = q_ref.shape[0]
    span = GROUP * HEAD_DIM
    pair = 2 * HEAD_DIM
    wide = HEAD_DIM // 2
    scale = HEAD_DIM**-0.5
    for blocks in range(1, kv_ref.shape[0] // rows + 1):

        @pl.when(shard_ref[0] == blocks - 1)
        def _():
            seen = blocks * rows
            key_grads = []
            for half in range(2):
                at = half * HEAD_DIM
                queries = q_ref[:, half * span : (half + 1) * span]
                grads = do_ref[:, half * span : (half + 1) * span]
                keys = kv_ref[:seen, at : at + HEAD_DIM]
                values = kv_ref[:seen, pair + at : pair + at + HEAD_DIM]
                queries_t = side_by_side(queries) * jnp.asarray(scale, BF)
                grads_t = side_by_side(grads)
                scores = causal_scores(keys, queries_t, rows, blocks)
                weights = jnp.exp(scores - lse_ref[0, half : half + 1, :])
                moved = mm(values, grads_t)
                product = weights * moved
                delta = jnp.sum(product, axis=0, keepdims=True)
                grad_scores = (product - weights * delta).astype(BF)
                dkv_ref[:seen, pair + at : pair + at + HEAD_DIM] = mm(
                    weights.astype(BF), stacked(grads)
                ).astype(BF)
                key_grads.append(mm(grad_scores, stacked(queries)) * scale)
                grad_t = mm(keys.T, grad_scores) * scale
                turned = []
                for h in range(GROUP):
                    block = grad_t[:, h * rows : (h + 1) * rows]
                    first, second = block[:wide], block[wide:]
                    turned.append(first * cos_ref[...] + second * sin_ref[...])
                    turned.append(second * cos_ref[...] - first * sin_ref[...])
                dq_ref[:, half * span : (half + 1) * span] = (
                    jnp.concatenate(turned, axis=0).T.astype(BF)
                )
            key_grads = jnp.concatenate(key_grads, axis=1)
            lane = lax.broadcasted_iota(jnp.int32, key_grads.shape, 1)
            dkv_ref[:seen, :pair] = turn(
                key_grads, kcos_ref[:seen, :], -ksin_ref[:seen, :], lane
            ).astype(BF)
            if seen < kv_ref.shape[0]:
                dkv_ref[seen:, :] = jnp.zeros((kv_ref.shape[0] - seen, 2 * pair), BF)


def attend_back(shard, queries, pairs, lse, grads, cosine, sine, key_cosine, key_sine):
    rows, width = queries.shape
    length, pair_width = pairs.shape
    steps = pair_width // (4 * HEAD_DIM)
    span = 2 * GROUP * HEAD_DIM
    table = pl.BlockSpec((HEAD_DIM // 2, rows), lambda p, s: (0, 0))
    key_table = pl.BlockSpec((length, LANES), lambda p, s: (0, 0))
    return pl.pallas_call(
        attend_back_kernel,
        grid_spec=pltpu.PrefetchScalarGridSpec(
            num_scalar_prefetch=1,
            grid=(steps,),
            in_specs=[
                pl.BlockSpec((rows, span), lambda p, s: (0, p)),
                pl.BlockSpec((length, 4 * HEAD_DIM), lambda p, s: (0, p)),
                pl.BlockSpec((1, 2, GROUP * rows), lambda p, s: (p, 0, 0)),
                pl.BlockSpec((rows, span), lambda p, s: (0, p)),
                table,
                table,
                key_table,
                key_table,
            ],
            out_specs=[
                pl.BlockSpec((rows, span), lambda p, s: (0, p)),
                pl.BlockSpec((length, 4 * HEAD_DIM), lambda p, s: (0, p)),
            ],
        ),
        out_shape=[
            jax.ShapeDtypeStruct((rows, width), BF),
            jax.ShapeDtypeStruct((length, pair_width), BF),
        ],
        compiler_params=pltpu.CompilerParams(vmem_limit_bytes=VMEM),
        cost_estimate=pl.CostEstimate(flops=1, bytes_accessed=1, transcendentals=0),
    )(shard, queries, pairs, lse, grads, cosine, sine, key_cosine, key_sine)


def widen_kernel(shard_ref, b_ref, *refs):
    gates, ups = refs[:4], refs[4:8]
    z_ref, g_ref, u_ref = refs[8:]
    depth = gates[0].shape[0]
    gate = up = None
    for k in range(4):
        at = pl.multiple_of((shard_ref[0] ^ k) * depth, depth)
        left = b_ref[:, pl.ds(at, depth)]
        g, u = mm(left, gates[k][...]), mm(left, ups[k][...])
        gate, up = (g, u) if gate is None else (gate + g, up + u)
    z_ref[...] = (gate * jax.nn.sigmoid(gate) * up).astype(BF)
    g_ref[...] = gate.astype(BF)
    u_ref[...] = up.astype(BF)


def widen(shard, b, gates, ups, tile=512):
    rows, width = b.shape
    depth, hidden = gates[0].shape
    out = pl.BlockSpec((rows, tile), lambda t, s: (0, t))
    return pl.pallas_call(
        widen_kernel,
        grid_spec=pltpu.PrefetchScalarGridSpec(
            num_scalar_prefetch=1,
            grid=(hidden // tile,),
            in_specs=[pl.BlockSpec((rows, width), lambda t, s: (0, 0))]
            + [pl.BlockSpec((depth, tile), lambda t, s: (0, t))] * 8,
            out_specs=[out] * 3,
        ),
        out_shape=[jax.ShapeDtypeStruct((rows, hidden), BF)] * 3,
        compiler_params=pltpu.CompilerParams(vmem_limit_bytes=VMEM),
        cost_estimate=pl.CostEstimate(flops=1, bytes_accessed=1, transcendentals=0),
    )(shard, b, *gates, *ups)


def narrow_kernel(shard_ref, z_ref, m_ref, *refs):
    downs, y_ref = refs[:4], refs[4]
    depth = downs[0].shape[0]
    total = m_ref[...]
    for k in range(4):
        at = pl.multiple_of((shard_ref[0] ^ k) * depth, depth)
        total = total + mm(z_ref[:, pl.ds(at, depth)], downs[k][...])
    y_ref[...] = total


def narrow(shard, z, m, downs, tile=256):
    rows, hidden = z.shape
    depth, width = downs[0].shape
    block = pl.BlockSpec((rows, tile), lambda t, s: (0, t))
    return pl.pallas_call(
        narrow_kernel,
        grid_spec=pltpu.PrefetchScalarGridSpec(
            num_scalar_prefetch=1,
            grid=(width // tile,),
            in_specs=[pl.BlockSpec((rows, hidden), lambda t, s: (0, 0)), block]
            + [pl.BlockSpec((depth, tile), lambda t, s: (0, t))] * 4,
            out_specs=block,
        ),
        out_shape=jax.ShapeDtypeStruct((rows, width), F32),
        compiler_params=pltpu.CompilerParams(vmem_limit_bytes=VMEM),
        cost_estimate=pl.CostEstimate(flops=1, bytes_accessed=1, transcendentals=0),
    )(shard, z, m, *downs)


def hidden_back_kernel(shard_ref, dy_ref, g_ref, u_ref, *refs):
    downs, gates, ups = refs[:4], refs[4:8], refs[8:12]
    dg_ref, du_ref, db_ref, total = refs[12:]
    step = pl.program_id(0)
    per = pl.num_programs(0) // 4
    depth = gates[0].shape[0]

    def one(down):
        dz = mm_nt(dy_ref[...], down[...])
        gate = g_ref[...].astype(F32)
        up = u_ref[...].astype(F32)
        slope = jax.nn.sigmoid(gate)
        dg = (dz * up * slope * (1.0 + gate * (1.0 - slope))).astype(BF)
        du = (dz * gate * slope).astype(BF)
        dg_ref[...] = dg
        du_ref[...] = du
        for k in range(4):
            part = mm_nt(dg, gates[k][...]) + mm_nt(du, ups[k][...])
            at = pl.multiple_of((shard_ref[0] ^ k) * depth, depth)

            @pl.when(step == 0)
            def _():
                total[:, pl.ds(at, depth)] = part

            @pl.when(step > 0)
            def _():
                total[:, pl.ds(at, depth)] += part

    for k in range(4):

        @pl.when(step // per == k)
        def _():
            one(downs[k])

    @pl.when(step == pl.num_programs(0) - 1)
    def _():
        db_ref[...] = total[...]


def hidden_back(shard, dy, g, u, downs, gates, ups, tile=512):
    rows, width = dy.shape
    hidden = g.shape[1]
    depth = gates[0].shape[0]
    per = hidden // 4 // tile

    def natural(t, s):
        return (0, (s[0] ^ (t // per)) * per + t % per)

    def piece(k):
        return lambda t, s: (jnp.clip(t - k * per, 0, per - 1), 0)

    cols = pl.BlockSpec((rows, tile), natural)
    whole = pl.BlockSpec((rows, width), lambda t, s: (0, 0))
    return pl.pallas_call(
        hidden_back_kernel,
        grid_spec=pltpu.PrefetchScalarGridSpec(
            num_scalar_prefetch=1,
            grid=(hidden // tile,),
            in_specs=[whole, cols, cols]
            + [pl.BlockSpec((tile, width), piece(k)) for k in range(4)]
            + [pl.BlockSpec((depth, tile), natural)] * 8,
            out_specs=[cols, cols, whole],
            scratch_shapes=[pltpu.VMEM((rows, width), F32)],
        ),
        out_shape=[
            jax.ShapeDtypeStruct((rows, hidden), BF),
            jax.ShapeDtypeStruct((rows, hidden), BF),
            jax.ShapeDtypeStruct((rows, width), F32),
        ],
        compiler_params=pltpu.CompilerParams(vmem_limit_bytes=VMEM),
        cost_estimate=pl.CostEstimate(flops=1, bytes_accessed=1, transcendentals=0),
    )(shard, dy, g, u, *downs, *gates, *ups)


def outer(x, row, parts, column, width, added=None, earlier=(), span=0, tile=512):
    per = (span or width) // tile
    count = width // tile // per
    first = column // tile
    at = row // CHUNK_ROWS
    held = [] if added is None else [added]
    extra = list(earlier)

    def kernel(*refs):
        step = pl.program_id(0)
        left = jnp.concatenate([part[...] for part in refs[: len(x)]], axis=1)
        refs = refs[len(x) :]
        right = jnp.concatenate([part[...] for part in refs[: len(parts)]], axis=0)
        value = mm(left, right)
        if held:
            value = value + refs[len(parts)][...].astype(F32)
        for index in range(count):

            @pl.when(step // per == index)
            def _():
                refs[len(parts) + len(held) + len(extra) + index][...] = value.astype(BF)

    def chunk(index):
        return lambda t: (0, jnp.clip(t - index * per, 0, per - 1))

    return pl.pallas_call(
        kernel,
        grid=(count * per,),
        in_specs=[pl.BlockSpec((CHUNK_ROWS, part.shape[1]), lambda t: (at, 0)) for part in x]
        + [pl.BlockSpec((part.shape[0], tile), lambda t: (0, first + t)) for part in parts]
        + [pl.BlockSpec((CHUNK_ROWS, tile), lambda t: (0, t))] * len(held)
        + [pl.BlockSpec(memory_space=pl.ANY)] * len(extra),
        out_specs=[pl.BlockSpec((CHUNK_ROWS, tile), chunk(index)) for index in range(count)],
        out_shape=[jax.ShapeDtypeStruct((CHUNK_ROWS, per * tile), BF)] * count,
        compiler_params=pltpu.CompilerParams(vmem_limit_bytes=VMEM),
        cost_estimate=pl.CostEstimate(flops=1, bytes_accessed=1, transcendentals=0),
    )(*x, *parts, *held, *extra)


def core_swap(x):
    return lax.ppermute(x, "fsdp", [(0, 1), (1, 0), (2, 3), (3, 2)])


def chip_swap(x):
    return lax.ppermute(x, "fsdp", [(0, 2), (2, 0), (1, 3), (3, 1)])


def after(value, other):
    always = lax.axis_index("dp") > -7
    return jnp.where(always, value, other.reshape(-1)[0].astype(value.dtype))


def nothing_kernel(*refs):
    pass


def hold(x, *others):
    anywhere = pl.BlockSpec(memory_space=pl.ANY)
    return pl.pallas_call(
        nothing_kernel,
        in_specs=[anywhere] * (1 + len(others)),
        out_specs=anywhere,
        out_shape=jax.ShapeDtypeStruct(x.shape, x.dtype),
        input_output_aliases={0: 0},
        compiler_params=pltpu.CompilerParams(vmem_limit_bytes=VMEM),
        cost_estimate=pl.CostEstimate(flops=1, bytes_accessed=1, transcendentals=0),
    )(x, *others)


def turned_kernel(shard_ref, *refs):
    for k in range(4):
        refs[4 + k][...] = refs[k][...].T


def turned_blocks(shard, x, tile=512):
    rows, width = x.shape
    per = width // 4 // tile

    def block(k):
        return pl.BlockSpec((rows, tile), lambda t, s: (0, (s[0] ^ k) * per + t))

    return pl.pallas_call(
        turned_kernel,
        grid_spec=pltpu.PrefetchScalarGridSpec(
            num_scalar_prefetch=1,
            grid=(per,),
            in_specs=[block(k) for k in range(4)],
            out_specs=[pl.BlockSpec((tile, rows), lambda t, s: (t, 0))] * 4,
        ),
        out_shape=[jax.ShapeDtypeStruct((width // 4, rows), x.dtype)] * 4,
        compiler_params=pltpu.CompilerParams(vmem_limit_bytes=VMEM),
        cost_estimate=pl.CostEstimate(flops=1, bytes_accessed=1, transcendentals=0),
    )(shard, x, x, x, x)


def column_block(x, index, width):
    return lax.dynamic_slice_in_dim(x, index * width, width, axis=1)


def relay_kernel(names, places, root, place_ref, *refs):
    named = dict(zip(names, refs))
    up_ref, down_ref = refs[-2:]
    place = place_ref[0]

    def read(name):
        return named[name][...].astype(F32) if name in named else 0.0

    own = 0.0
    for name, held_by in places:
        if name not in named:
            continue
        mine = held_by[0] == place
        for position in held_by[1:]:
            mine = mine | (place == position)
        own = jnp.where(mine, named[name][...].astype(F32), own)
    total = own + read("below_held") + read("above_held")
    up = jnp.where(place == root, total, read("below") + jnp.where(place < root, own, 0.0))
    down = jnp.where(place == root, total, read("above") + jnp.where(place > root, own, 0.0))
    up_ref[...] = jnp.broadcast_to(up, up_ref.shape).astype(up_ref.dtype)
    down_ref[...] = jnp.broadcast_to(down, down_ref.shape).astype(down_ref.dtype)


def relay(place, root, places, operands, earlier, shape, kind):
    names = [name for name in operands if operands[name] is not None]
    unique, at = [], {}
    for name in names:
        for index, other in enumerate(unique):
            if operands[name] is other:
                at[name] = index
        if name not in at:
            at[name] = len(unique)
            unique.append(operands[name])
    rows, cols = shape
    tile = rows // 2 if rows >= 256 else rows
    block = pl.BlockSpec((tile, cols), lambda t, s: (t, 0))

    def kernel(place_ref, *refs):
        values = refs[: len(unique)]
        relay_kernel(names, places, root, place_ref, *[values[at[n]] for n in names], *refs[-2:])

    return pl.pallas_call(
        kernel,
        grid_spec=pltpu.PrefetchScalarGridSpec(
            num_scalar_prefetch=1,
            grid=(rows // tile,),
            in_specs=[block] * len(unique) + [pl.BlockSpec(memory_space=pl.ANY)] * len(earlier),
            out_specs=[block, block],
        ),
        out_shape=[jax.ShapeDtypeStruct(shape, kind)] * 2,
        compiler_params=pltpu.CompilerParams(vmem_limit_bytes=VMEM),
        cost_estimate=pl.CostEstimate(flops=1, bytes_accessed=1, transcendentals=0),
    )(place, *unique, *earlier)


def replica_chain(count, make, shape, kind, stream_count=STREAMS, wanted=None, done=None):
    peers = lax.axis_size("dp")
    place = lax.axis_index("dp")
    place_vector = place.astype(jnp.int32).reshape(1)
    root = (peers - 1) // 2
    delay = max(root, peers - 1 - root)
    counts = [len(range(q, count, stream_count)) for q in range(stream_count)]
    streams = [[] for _ in counts]
    ups = [[] for _ in streams]
    downs = [[] for _ in streams]
    sent = [[] for _ in streams]
    order = []
    tokens = []
    choice = 2 * jnp.abs(place - root) + (place < root).astype(jnp.int32)
    choice = choice.astype(jnp.int32).reshape(1)
    found = []
    lags = [
        position if position < root else delay if position == root else peers - 1 - position
        for position in range(peers)
    ]

    def nth(items, index):
        return items[index] if 0 <= index < len(items) else None

    def going(position, direction, step):
        if (root - position) * direction > 0:
            return step - lags[position]
        return step - delay - abs(position - root)

    for step in range(max(counts) + 2 * delay):
        for q in range(stream_count):
            if step >= counts[q] + 2 * delay:
                continue
            if wanted is not None and order:
                wanted(len(order), order[-1][0])
            if step < counts[q]:
                before = (order[-LEAD][0],) if len(order) >= LEAD else ()
                streams[q].append(make(q + step * stream_count, before))
            places, operands = [], {}
            for lag in sorted(set(lags)):
                name = f"own{lag}"
                operands[name] = nth(streams[q], step - lag)
                places.append((name, [p for p in range(peers) if lags[p] == lag]))
            operands["below"] = nth(ups[q], step - 1)
            operands["above"] = nth(downs[q], step - 1)
            operands["below_held"] = nth(ups[q], step - 1 - (delay - root))
            operands["above_held"] = nth(downs[q], step - 1 - (delay - (peers - 1 - root)))
            earlier = ()
            if stream_count > 1 and len(order) > stream_count:
                earlier = order[-(stream_count + 1)]
            if len(tokens) >= 2:
                earlier = (*earlier, tokens[-2])
            up, down = relay(place_vector, root, places, operands, earlier, shape, kind)
            sent[q].append((up, down))
            at = step - 2 * delay
            if at >= 0:
                found = [x for hops in range(delay + 1) for x in sent[q][at + delay + hops]]
                token = done(q + at * stream_count, choice, found)
                if token is not None:
                    tokens.append(token)
            if step < counts[q] + 2 * delay - 1:
                up_pairs = [(i, i + 1) for i in range(peers - 1) if 0 <= going(i, 1, step) < counts[q]]
                down_pairs = [(i, i - 1) for i in range(1, peers) if 0 <= going(i, -1, step) < counts[q]]
                ups[q].append(lax.ppermute(up, "dp", up_pairs))
                downs[q].append(lax.ppermute(down, "dp", down_pairs))
                order.append((ups[q][-1], downs[q][-1]))


def place_chunk(choice, found, whole, shape, row, column, tile=128):
    per = CHUNK_ROWS // tile
    kept = [] if whole is None else [whole]

    def kernel(choice_ref, *refs):
        for index in range(len(found)):

            @pl.when(choice_ref[0] == index)
            def _():
                refs[-2][...] = refs[index][...].astype(F32)

        refs[-1][...] = jnp.zeros(refs[-1].shape, F32)

    def chosen(index):
        return lambda t, s: (jnp.where(s[0] == index, t, 0), 0)

    return pl.pallas_call(
        kernel,
        grid_spec=pltpu.PrefetchScalarGridSpec(
            num_scalar_prefetch=1,
            grid=(per,),
            in_specs=[pl.BlockSpec((tile, CHUNK_COLS), chosen(k)) for k in range(len(found))]
            + [pl.BlockSpec(memory_space=pl.ANY)] * len(kept),
            out_specs=[
                pl.BlockSpec((tile, CHUNK_COLS), lambda t, s: (row * per + t, column)),
                pl.BlockSpec((8, LANES), lambda t, s: (0, 0)),
            ],
        ),
        out_shape=[
            jax.ShapeDtypeStruct(shape, F32),
            jax.ShapeDtypeStruct((8, LANES), F32),
        ],
        input_output_aliases={1 + len(found): 0} if kept else {},
        compiler_params=pltpu.CompilerParams(vmem_limit_bytes=VMEM),
        cost_estimate=pl.CostEstimate(flops=1, bytes_accessed=1, transcendentals=0),
    )(choice, *found, *kept)


def body(
    ends, positions, attn_gain, w_query, w_key, w_value, w_out, mlp_gain, w_gate, w_up, w_down
):
    shard = lax.axis_index("fsdp")
    shard_vector = shard.astype(jnp.int32).reshape(1)
    replica = lax.axis_index("dp")
    replicas = lax.axis_size("dp")
    first_section = lax.axis_index("section") == 0
    tok_rows = ends.shape[3]
    model_width = ends.shape[4]
    length = tok_rows * lax.axis_size("fsdp")
    key_width = w_key.shape[2]
    query_width = w_query.shape[2]
    ends_local = ends[0, :, 0]

    gains = lax.all_gather(
        jnp.concatenate([attn_gain, mlp_gain], axis=0), "fsdp", axis=1, tiled=True
    ).astype(F32)
    gain_attn, gain_mlp = gains[0], gains[1]
    places_all = lax.all_gather(positions[:, 0], "fsdp", axis=1, tiled=True)
    start = gain_attn[0] + places_all[0, 0].astype(F32)

    def rotary(micro_first, micro_second):
        places = jnp.where(first_section, places_all[micro_first], places_all[micro_second])
        half = HEAD_DIM // 2
        frequency = jnp.exp(-jnp.log(ROPE_THETA) * 2.0 * jnp.arange(half, dtype=F32) / HEAD_DIM)
        angles = places.astype(F32)[:, None] * frequency[None, :]
        cosine, sine = jnp.cos(angles), jnp.sin(angles)
        own = [lax.dynamic_slice_in_dim(x, shard * tok_rows, tok_rows, 0) for x in (cosine, sine)]
        lanes = LANES // HEAD_DIM
        wide = (
            jnp.tile(cosine, (1, 2 * lanes)),
            jnp.tile(jnp.concatenate([-sine, sine], axis=1), (1, lanes)),
        )
        wide_own = [lax.dynamic_slice_in_dim(x, shard * tok_rows, tok_rows, 0) for x in wide]
        return wide_own, (own[0].T, own[1].T), wide

    table_a = rotary(1, 0)
    table_b = rotary(0, 1)

    def part(x):
        rows = x.shape[0] // replicas
        return lax.dynamic_slice_in_dim(x, replica * rows, rows, axis=0)

    def spread(x):
        return lax.all_gather(x, "dp", axis=0, tiled=True)

    pieces = [w_query[0]]
    for at in range(0, key_width, LANES):
        pieces += [w_key[0, :, at : at + LANES], w_value[0, :, at : at + LANES]]
    own_qkv = jnp.concatenate(pieces, axis=1)
    own_out, own_gate, own_up, own_down = w_out[0], w_gate[0], w_up[0], w_down[0]
    middle = own_gate.shape[1] // 2
    sends = [part(own_gate[:, :middle]), own_qkv, part(own_gate[:, middle:])]
    sends += [part(own_out), part(own_up)]
    got = []
    spreads = []
    for index, send in enumerate(sends):
        send = after(send, got[-1] if got else start)
        if index == 4:
            send = after(send, spreads[0])
        got.append(chip_swap(send))
        if index != 1:
            spreads.append(spread(got[-1]))

    def shards(own, other):
        return (own, core_swap(own), other, core_swap(other))

    def natural(values):
        rows = values[0].shape[0]
        whole = jnp.zeros((4 * rows, values[0].shape[1]), BF)
        for k, value in enumerate(values):
            whole = lax.dynamic_update_slice(whole, value, ((shard ^ k) * rows, 0))
        return whole

    gates = shards(own_gate, jnp.concatenate(spreads[:2], axis=1))
    mat_qkv = natural(shards(own_qkv, got[1]))
    mat_out = natural(shards(own_out, spreads[2]))

    def all_rows(x):
        return shards(x, chip_swap(x))

    def summed_rows(x):
        def rows_of(index):
            return lax.dynamic_slice_in_dim(x, index * tok_rows, tok_rows, 0)

        near = rows_of(shard).astype(F32) + core_swap(rows_of(shard ^ 1)).astype(F32)
        far = rows_of(shard ^ 2).astype(F32) + core_swap(rows_of(shard ^ 3)).astype(F32)
        return (near + chip_swap(far.astype(BF)).astype(F32)).astype(BF)

    def enter(layer_input, table):
        inverse_one = rms_inverse(layer_input)
        normed_attn = (layer_input * inverse_one * gain_attn).astype(BF)
        queries, pairs = project(normed_attn, mat_qkv, *table[0], key_width)
        return inverse_one, normed_attn, queries, natural(all_rows(pairs))

    def middle_part(layer_input, entered, *waits):
        held = shard_vector
        for other in waits:
            held = after(held, other)
        attended, log_totals = attend(held, entered[2], entered[3])
        residual_mid = layer_input + mm(attended, mat_out)
        inverse_two = rms_inverse(residual_mid)
        normed_mlp = (residual_mid * inverse_two * gain_mlp).astype(BF)
        return attended, log_totals, residual_mid, inverse_two, normed_mlp

    def leave(layer_input, entered, halfway, widened=None):
        inverse_one, normed_attn, queries, pairs_all = entered
        attended, log_totals, residual_mid, inverse_two, normed_mlp = halfway
        widened = widened or widen(shard_vector, normed_mlp, gates, ups)
        hidden_act, gate_pre, up_proj = widened
        output = narrow(shard_vector, hidden_act, residual_mid, downs)
        return output, {
            "input": layer_input,
            "inverse_one": inverse_one,
            "a": normed_attn,
            "queries": queries,
            "pairs": pairs_all,
            "log": log_totals,
            "o": attended,
            "mid": residual_mid,
            "inverse_two": inverse_two,
            "b": normed_mlp,
            "gate": gate_pre,
            "up": up_proj,
            "z": hidden_act,
        }

    def back_upper(grad_top, saved):
        grad_gate_pre, grad_up_proj, grad_normed = hidden_back(
            shard_vector, grad_top, saved["gate"], saved["up"], downs, gates, ups
        )
        inverse_two = saved["inverse_two"]
        base_mid = saved["mid"] * inverse_two
        part_gain_mlp = jnp.sum(grad_normed * base_mid, axis=0)
        scaled_grad = grad_normed * gain_mlp
        grad_mid = grad_top.astype(F32) + inverse_two * (
            scaled_grad - base_mid * jnp.mean(scaled_grad * base_mid, axis=-1, keepdims=True)
        )
        attn_grad = grad_mid.astype(BF)
        return grad_gate_pre, grad_up_proj, attn_grad, grad_mid, part_gain_mlp

    def back_attention(upper, saved, table, *waits):
        held = shard_vector
        for other in waits:
            held = after(held, other)
        grad_attended = mm_nt(upper[2], mat_out).astype(BF)
        grad_queries, grad_pairs = attend_back(
            held, saved["queries"], saved["pairs"], saved["log"], grad_attended, *table[1], *table[2]
        )

        def rows_of(index):
            return lax.dynamic_slice_in_dim(grad_pairs, index * tok_rows, tok_rows, 0)

        far = rows_of(shard ^ 2).astype(F32) + core_swap(rows_of(shard ^ 3)).astype(F32)
        far = far.astype(BF)
        near = rows_of(shard).astype(F32) + core_swap(rows_of(shard ^ 1)).astype(F32)
        return grad_queries, near, far

    def back_lower(upper, attention, saved, far=None):
        grad_queries, near, sent = attention
        far = chip_swap(sent) if far is None else far
        grad_qkv = jnp.concatenate([grad_queries, (near + far.astype(F32)).astype(BF)], axis=1)
        grad_normed = mm_nt(grad_qkv, mat_qkv)
        base_in = saved["input"] * saved["inverse_one"]
        part_gain_attn = jnp.sum(grad_normed * base_in, axis=0)
        scaled_grad = grad_normed * gain_attn
        grad_in = upper[3] + saved["inverse_one"] * (
            scaled_grad - base_in * jnp.mean(scaled_grad * base_in, axis=-1, keepdims=True)
        )
        return grad_in, grad_qkv, jnp.stack([part_gain_attn, upper[4]])

    def ahead(x):
        return lax.ppermute(x.astype(BF), "section", [(0, 1)])

    def back(x):
        return lax.ppermute(x.astype(BF), "section", [(1, 0)])

    def choose(first, second):
        return jnp.where(first_section, first, second)

    layer_input = ends_local[0].astype(F32)
    entered = enter(layer_input, table_b)
    other_down = chip_swap(after(after(own_down, got[-1]), entered[3]))
    halfway = middle_part(layer_input, entered)
    ups = shards(own_up, hold(spreads[3], halfway[4]))
    downs = shards(own_down, hold(other_down, halfway[4]))
    output, _ = leave(layer_input, entered, halfway)
    received = ahead(output)
    layer_input = choose(ends_local[1], received).astype(F32)
    entered = enter(layer_input, table_a)
    output_one, saved_a = leave(layer_input, entered, middle_part(layer_input, entered))
    received = ahead(output_one)
    turned_a = turned_blocks(shard_vector, saved_a["z"])
    layer_input = choose(ends_local[0], received).astype(F32)
    entered = enter(layer_input, table_b)
    halfway = middle_part(layer_input, entered, turned_a[0])
    output_two, saved_b = leave(layer_input, entered, halfway)
    turned_b = turned_blocks(shard_vector, saved_b["z"])

    def shares(blocks_a, blocks_b):
        near = (blocks_a[0], blocks_b[0], core_swap(blocks_a[1]), core_swap(blocks_b[1]))
        far = (blocks_a[2], blocks_b[2], core_swap(blocks_a[3]), core_swap(blocks_b[3]))
        return near, far

    def shares_of(name):
        return shares(
            turned_blocks(shard_vector, saved_a[name]), turned_blocks(shard_vector, saved_b[name])
        )

    def chip_rows(first, second):
        return (first, second, core_swap(first), core_swap(second))

    upper = back_upper(ends_local[0], saved_a)
    grad_in, _, _ = back_lower(upper, back_attention(upper, saved_a, table_a), saved_a)
    received = back(grad_in)
    top_b = choose(received, ends_local[1])
    upper_b = back_upper(top_b, saved_b)
    attention = back_attention(upper_b, saved_b, table_b)
    grad_one, grad_qkv_b, gains_b = back_lower(upper_b, attention, saved_b)
    received = back(grad_one)
    shared = {name: shares_of(name) for name in ("b", "o", "a")}
    received = hold(received, output_two, *[shared[name][1][0] for name in ("b", "o", "a")])
    top_a = choose(received, ends_local[0])

    late = {"down": (shares(turned_a, turned_b), chip_rows(top_a, top_b))}
    work = {}
    crossed = []

    def begin_last(begun):
        work["upper"] = upper_a = back_upper(after(top_a, begun), saved_a)
        late["gate"] = (shared["b"], chip_rows(upper_a[0], upper_b[0]))
        late["up"] = (shared["b"], chip_rows(upper_a[1], upper_b[1]))
        late["out"] = (shared["o"], chip_rows(upper_a[2], upper_b[2]))

    def wanted(sends, last):
        if sends == ATTEND_AT:
            work["attention"] = back_attention(work["upper"], saved_a, table_a, last)
        if sends == LOWER_AT:
            far = crossed[FAR_WITH][CHUNK_ROWS:, : work["attention"][2].shape[1]]
            work["done"] = back_lower(work["upper"], work["attention"], saved_a, far)
            late["attn"] = (shared["a"], chip_rows(work["done"][1], grad_qkv_b))
            gains = work["done"][2] + gains_b
            gains = (gains + core_swap(gains)).astype(BF)
            block = model_width // 4
            own, other = column_block(gains, shard, block), column_block(gains, shard ^ 2, block)
            gains = own.astype(F32) + chip_swap(other).astype(F32)
            spare = ((0, CHUNK_ROWS - gains.shape[0]), (0, CHUNK_COLS - block))
            work["gains"] = jnp.pad(gains, spare).astype(BF)

    pair = 2 * CHUNK_COLS
    hidden_width = w_gate.shape[2]
    qkv_width = query_width + 2 * key_width
    plan = []
    for row in range(0, w_down.shape[1], CHUNK_ROWS):
        plan += [("down", row, col, pair) for col in range(0, model_width, pair)]
    for name, width in (("gate", hidden_width), ("up", hidden_width), ("out", model_width)):
        plan += [(name, 0, col, pair) for col in range(0, width, pair)]
    plan += [("attn", 0, col, min(pair, qkv_width - col)) for col in range(0, qkv_width, pair)]
    made = []

    def cross(earlier):
        name, row, col, width = plan[len(crossed)]
        (own, other), parts = late[name]
        (result,) = outer(other, row, parts, col, width, None, earlier)
        if len(crossed) == FAR_WITH:
            far = work["attention"][2]
            far = jnp.pad(far, ((0, 0), (0, result.shape[1] - far.shape[1])))
            result = jnp.concatenate([result, far], axis=0)
        crossed.append(chip_swap(result))
        return result

    def make(index, earlier):
        if index == count - 1:
            return work["gains"]
        if index == len(made):
            at = index // 2
            if index == 0:
                cross(())
                begin_last(cross(()))
                earlier = (work["upper"][0],)
            name, row, col, width = plan[at]
            (own, other), parts = late[name]
            made.extend(outer(own, row, parts, col, width, crossed[at], earlier, CHUNK_COLS))
        elif len(crossed) < len(plan):
            cross(earlier)
        return made[index]

    count = sum(width // CHUNK_COLS for _, _, _, width in plan) + 1
    results = {}
    table = []
    for name, rows, cols in (
        ("down", w_down.shape[1], w_down.shape[2]),
        ("gate", w_gate.shape[1], w_gate.shape[2]),
        ("up", w_up.shape[1], w_up.shape[2]),
        ("out", w_out.shape[1], w_out.shape[2]),
        ("query", w_query.shape[1], query_width),
        ("pairs", w_query.shape[1], 2 * key_width),
    ):
        for row in range(rows // CHUNK_ROWS):
            for column in range(cols // CHUNK_COLS):
                table.append((name, (rows, cols), row, column))

    def done(index, choice, found):
        if index == count - 1:
            last = [x[: gains_b.shape[0], : model_width // 4] for x in found]
            gains = last[0]
            for at, x in enumerate(last):
                gains = jnp.where(choice[0] == at, x, gains)
            results["gains"] = gains.astype(F32)
            return None
        name, shape, row, column = table[index]
        whole = results.get(name)
        results[name], token = place_chunk(choice, found, whole, shape, row, column)
        return token

    replica_chain(count, make, (CHUNK_ROWS, CHUNK_COLS), BF, wanted=wanted, done=done)
    grad_two = work["done"][0]
    gains = results["gains"]
    grad_down, grad_gate, grad_up = results["down"], results["gate"], results["up"]
    grad_out, grad_query, grad_both = results["out"], results["query"], results["pairs"]
    grad_pairs = [grad_both[:, at : at + LANES] for at in range(0, 2 * key_width, LANES)]
    boundary = choose(jnp.stack([grad_one, grad_two]), jnp.stack([output_one, output_two]))
    return (
        boundary[None, :, None],
        gains[0][None],
        grad_query[None],
        jnp.concatenate(grad_pairs[::2], axis=1)[None],
        jnp.concatenate(grad_pairs[1::2], axis=1)[None],
        grad_out[None],
        gains[1][None],
        grad_gate[None],
        grad_up[None],
        grad_down[None],
    )


def solution(mesh):
    weight = P("section", "fsdp", None)
    gain = P("section", "fsdp")
    ends = P("section", None, "dp", "fsdp", None)
    return jax.shard_map(
        body,
        mesh=mesh,
        in_specs=(
            ends,
            P(None, "dp", "fsdp"),
            gain,
            weight,
            weight,
            weight,
            weight,
            gain,
            weight,
            weight,
            weight,
        ),
        out_specs=(
            ends,
            gain,
            weight,
            weight,
            weight,
            weight,
            gain,
            weight,
            weight,
            weight,
        ),
        check_vma=False,
    )
```
